128 devices in a mesh: graph: 16 (over x, z), leaf: 8 (over y, core).
Axes of the slice: x: 4, y: 4, z: 4, core: 2. Of those that a mesh axis runs over, the one named last changes fastest.
Arguments:
- features: bfloat16 [32768, 384], P(('graph', 'leaf')), may hold values from -6 to 6
- send_rows: int32 [128, 128, 32], P(('graph', 'leaf')), may hold values from 0 to 255
- neighbour_slot: int32 [32768, 16], P(('graph', 'leaf')), may hold values from 0 to 4095, as said below
- degree: int32 [32768], P(('graph', 'leaf')), may hold values from 1 to 16
- self_weight: bfloat16 [384, 512], replicated, may hold values from -0.3125 to 0.3125
- neigh_weight: bfloat16 [384, 512], replicated, may hold values from -0.3125 to 0.3125
- hidden_bias: float32 [512], replicated, may hold values from -3 to 3
- out_weight: bfloat16 [512, 64], replicated, may hold values from -0.25 to 0.25
- out_bias: float32 [64], replicated, may hold values from -3 to 3
- out_gain: float32 [64], replicated, may hold values from 0.25 to 1.75
- split_feature: int32 [512, 63], P('leaf'), may hold values from 0 to 447
- threshold: float32 [512, 63], P('leaf'), may hold values from -1 to 1
- leaf_value: float32 [512, 64], P('leaf'), may hold values from -0.6 to 0.6
Outputs:
- embedding: bfloat16 [32768, 64], P(('graph', 'leaf'))
- fraud_score: float32 [32768], P(('graph', 'leaf'))
The draws below stay inside these ranges and needn't reach their ends.
Inputs may be any that keep to these rules, and one draw needn't show every extreme that they name: `neighbour_slot`: entry [i, j] is a slot s * 32 + k of the buffer that card i's device receives. The slots that one device's cards name from one source s are among the first c of that source, c from 1 to 32 depending on the pair. Only the first degree[i] entries of row i of neighbour_slot count.
All inputs are finite; a program needn't handle non-finite values.
Results may differ from the reference program's by a relative error of at most 0.0047.
Values may be sent and summed in bfloat16 or wider, within the bound.
A program may use at most 64 MiB of HBM per device.

```python
import jax
import jax.numpy as jnp
from jax import lax

F_IN = 384
HID = 512
EMB = 64
DEPTH = 6
KNB = 16
ROWS = 256
CAP = 32
SLOTS = 4096
CARDS = 32768
TREES = 512
LEAVES = 64
INNER = 63
FEAT = 448
DEVICES = 128


def draw_neighbour_slot(key, part):
    count_key, heat_key, forced_key, pick_key = jax.random.split(jax.random.fold_in(key, 17), 4)
    heat_draw = jax.random.randint(heat_key, (DEVICES,), 0, 16)
    forced = jax.random.randint(forced_key, (), 0, DEVICES)
    hot_targets = jnp.logical_or(heat_draw == 0, jnp.arange(DEVICES) == forced)
    lowest = max(1, CAP // 8)
    base_counts = jax.random.randint(count_key, (DEVICES, DEVICES), lowest, CAP // 2 + 1)
    counts = jnp.where(hot_targets[None, :], CAP, base_counts)
    totals = jnp.sum(counts, axis=0)
    cumulative = jnp.cumsum(counts, axis=0)
    pick_draw = jax.random.randint(pick_key, (DEVICES, ROWS, KNB), 0, totals[:, None, None])

    def per_device(inputs):
        device_picks, device_cum, device_counts = inputs
        source = jnp.sum((device_cum[None, None, :] <= device_picks[:, :, None]).astype(jnp.int32), axis=2)
        start_of = jnp.take(device_cum - device_counts, source)
        return source * CAP + device_picks - start_of
    slot_ids = lax.map(per_device, (pick_draw, cumulative.T, counts.T)).reshape(CARDS, KNB)
    return slot_ids.at[forced * ROWS, 0].set(SLOTS - 1)


def place_ends(entries, key, low, largest):
    spot = [jax.random.randint(jax.random.fold_in(key, axis), (), 0, length) for axis, length in enumerate(entries.shape)]
    main_axis = entries.shape.index(max(entries.shape))
    neighbour = spot[:main_axis] + [(spot[main_axis] + 1) % entries.shape[main_axis]] + spot[main_axis + 1:]
    return entries.at[tuple(spot)].set(low).at[tuple(neighbour)].set(largest)


def steps_of(key, shape, cuts, low, high):
    def one(axis_at, parts):
        heights = jax.random.uniform(jax.random.fold_in(jax.random.fold_in(key, 6), axis_at), (parts,), jnp.float32, low / len(cuts), high / len(cuts))
        return jnp.repeat(jnp.exp(heights), shape[axis_at] // parts).reshape((-1,) + (1,) * (len(shape) - axis_at - 1))

    level = one(*cuts[0])
    for cut in cuts[1:]:
        level = level * one(*cut)
    return level


def gaussian(rng, dims, width, limit, shards=(), kind=jnp.bfloat16):
    values = jax.random.normal(rng, dims, jnp.float32) * width
    if len(shards) > 0:
        values = steps_of(rng, dims, shards, -0.22, 0.18) * values
    return jnp.clip(values, min=-limit, max=limit).astype(kind)


def setup_inputs(seed: int = 0) -> dict:
    splits = jax.random.split(jax.random.key(seed), 14)
    features = gaussian(splits[0], (CARDS, F_IN), 1.0, 6.0, ((0, 128),))
    send_rows = place_ends(jax.random.randint(splits[1], (DEVICES, DEVICES, CAP), 0, ROWS), jax.random.fold_in(splits[1], 1), 0, ROWS - 1).astype(jnp.int32)
    neighbour_slot = draw_neighbour_slot(jax.random.fold_in(splits[13], 71), 0)
    degree = place_ends(jax.random.randint(splits[3], (CARDS,), 1, KNB + 1), jax.random.fold_in(splits[3], 1), 1, KNB).astype(jnp.int32)
    self_weight = gaussian(splits[4], (F_IN, HID), F_IN ** -0.5, 0.3125)
    neigh_weight = gaussian(splits[5], (F_IN, HID), F_IN ** -0.5, 0.3125)
    hidden_bias = gaussian(splits[6], (HID,), 0.5, 3.0, (), jnp.float32)
    out_weight = gaussian(splits[7], (HID, EMB), HID ** -0.5, 0.25)
    out_bias = gaussian(splits[8], (EMB,), 0.5, 3.0, (), jnp.float32)
    out_gain = jnp.clip(1.0 + 0.15 * jax.random.normal(splits[9], (EMB,), jnp.float32), 0.25, 1.75)
    split_feature = place_ends(jax.random.randint(splits[10], (TREES, INNER), 0, FEAT), jax.random.fold_in(splits[10], 1), 0, FEAT - 1).astype(jnp.int32)
    threshold = jnp.clip(jax.random.uniform(splits[11], (TREES, INNER), jnp.float32, -1.0, 1.0) * steps_of(splits[11], (TREES, INNER), ((0, 8),), -0.4, 0.0), -1.0, 1.0)
    leaf_value = gaussian(splits[12], (TREES, LEAVES), 0.1, 0.6, ((0, 8),), jnp.float32)
    return dict(features=features, send_rows=send_rows, neighbour_slot=neighbour_slot, degree=degree, self_weight=self_weight, neigh_weight=neigh_weight, hidden_bias=hidden_bias, out_weight=out_weight, out_bias=out_bias, out_gain=out_gain, split_feature=split_feature, threshold=threshold, leaf_value=leaf_value)


SHARPNESS = 2.0
NORM_EPS = 1e-05

def sage_rows(own_rows, picked, own_degree, self_weight, neigh_weight, hidden_bias, out_weight, out_bias, out_gain):
    counted = (lax.broadcasted_iota(jnp.int32, picked.shape[:2], 1) < own_degree[:, None]).astype(jnp.float32)
    summed = jnp.einsum('rk,rkf->rf', counted, picked.astype(jnp.float32), precision=lax.Precision.HIGHEST)
    neigh_mean = (summed / own_degree[:, None].astype(jnp.float32)).astype(jnp.bfloat16)
    own_term = jnp.dot(own_rows, self_weight, preferred_element_type=jnp.float32)
    hidden = jax.nn.relu(own_term + jnp.dot(neigh_mean, neigh_weight, preferred_element_type=jnp.float32) + hidden_bias).astype(jnp.bfloat16)
    raw_embed = jnp.dot(hidden, out_weight, preferred_element_type=jnp.float32) + out_bias
    scaled = raw_embed * lax.rsqrt(lax.optimization_barrier(jnp.mean(raw_embed * raw_embed, axis=1, keepdims=True)) + NORM_EPS)
    return (scaled * out_gain).astype(jnp.bfloat16)

def forest_scores(vectors, split_feature, threshold, leaf_value):
    tree_total, inner_total = split_feature.shape

    def score_block(row_block):
        row_total = row_block.shape[0]
        chosen = jnp.take(row_block, split_feature.reshape(-1), axis=1).astype(jnp.float32)
        margin = (chosen.reshape(row_total, tree_total, inner_total) - threshold[None]) * SHARPNESS
        log_reach = jnp.zeros((row_total, tree_total, 1), jnp.float32)
        for height in range(DEPTH):
            first_node = 2 ** height - 1
            level_margin = margin[:, :, first_node:first_node + 2 ** height]
            go_left = log_reach + jax.nn.log_sigmoid(-level_margin)
            go_right = log_reach + jax.nn.log_sigmoid(level_margin)
            log_reach = jnp.stack([go_left, go_right], axis=-1).reshape(row_total, tree_total, 2 ** (height + 1))
        return jnp.einsum('rtl,tl->r', jnp.exp(log_reach), leaf_value, precision=lax.Precision.HIGHEST)
    return lax.map(score_block, vectors.reshape(DEVICES, ROWS, vectors.shape[1])).reshape(-1)

def reference(features, send_rows, neighbour_slot, degree, self_weight, neigh_weight, hidden_bias, out_weight, out_bias, out_gain, split_feature, threshold, leaf_value):
    sources = jnp.arange(DEVICES, dtype=jnp.int32)[:, None, None] * ROWS + send_rows
    sources = jnp.transpose(sources, (1, 0, 2)).reshape(DEVICES, SLOTS)
    slot_blocks = neighbour_slot.reshape(DEVICES, ROWS, KNB)
    degree_blocks = degree.reshape(DEVICES, ROWS)
    feature_blocks = features.reshape(DEVICES, ROWS, F_IN)

    def embed_block(inputs):
        own_rows, own_slots, own_degree, own_sources = inputs
        global_rows = jnp.take(own_sources, own_slots, axis=0)
        picked = jnp.take(features, global_rows, axis=0)
        return sage_rows(own_rows, picked, own_degree, self_weight, neigh_weight, hidden_bias, out_weight, out_bias, out_gain)
    embedding = lax.map(embed_block, (feature_blocks, slot_blocks, degree_blocks, sources)).reshape(CARDS, EMB)
    vectors = jnp.concatenate([features, embedding], axis=1)
    fraud_score = forest_scores(vectors, split_feature, threshold, leaf_value)
    return (embedding, fraud_score)
```

```python
import functools

import jax
import jax.numpy as jnp
from jax import lax
from jax.experimental import pallas as pl
from jax.experimental.pallas import tpu as pltpu
from jax.sharding import PartitionSpec as P

NORM_EPS = 1e-05
CAP = 32
GROUP = 16
BF16 = jnp.bfloat16
F32 = jnp.float32
MESH = pl.DeviceIdType.MESH


def post_order(inner):
    order = []

    def visit(node):
        if node < inner:
            visit(2 * node + 1)
            visit(2 * node + 2)
            order.append(node)

    visit(0)
    place = [0] * inner
    for position, node in enumerate(order):
        place[node] = position
    return place


def flip(a, b, size):
    total = 0
    bit = 1
    while bit < size:
        total = total + ((a // bit + b // bit) % 2) * bit
        bit *= 2
    return total


def kernel(
    graphs,
    leaves,
    features,
    send_rows,
    neighbour_slot,
    degree,
    self_weight,
    neigh_weight,
    hidden_bias,
    out_weight,
    out_bias,
    out_gain,
    split_feature,
    threshold,
    leaf_value,
    embedding,
    scores,
    feats,
    ids,
    outgoing,
    arrived,
    slot_ids,
    counts,
    selector,
    leaf_mid,
    leaf_half,
    inputs_t,
    own_term,
    out_weight_t,
    out_cols,
    degree_col,
    summed,
    partial,
    partial_in,
    feat_send,
    ids_send,
    row_send,
    emb_send,
    score_send,
    feat_recv,
    ids_recv,
    row_recv,
    emb_recv,
    score_recv,
):
    g = lax.axis_index("graph")
    m = lax.axis_index("leaf")
    rows, f_in = features.shape
    trees, inner = split_feature.shape
    emb = out_weight.shape[1]
    entries = neighbour_slot.shape[1]
    width = leaves * CAP
    groups = trees // GROUP
    place = post_order(inner)
    lanes = lax.broadcasted_iota(jnp.int32, (1, 128), 1)

    barrier = pltpu.get_barrier_semaphore()

    @pl.loop(1, graphs)
    def _(step):
        pl.semaphore_signal(
            barrier, inc=1, device_id=(lax.rem(g + step, graphs), m), device_id_type=MESH
        )

    @pl.loop(1, leaves)
    def _(step):
        pl.semaphore_signal(
            barrier, inc=1, device_id=(g, flip(m, step, leaves)), device_id_type=MESH
        )

    devices = graphs * leaves
    wide = jnp.concatenate([send_rows[...], jnp.zeros((devices, 128 - CAP), jnp.int32)], axis=1)
    ids[0] = wide.T[:CAP]
    feats[0] = features[...]
    pl.semaphore_wait(barrier, graphs - 1 + leaves - 1)

    def leaf_order(i):
        if leaves == 8:
            return i + 2 * ((i // 4) * (1 - 2 * ((i // 2) % 2)))
        return i

    @pl.loop(1, leaves)
    def _(i):
        p = leaf_order(i)
        peer = (g, flip(m, p, leaves))
        pltpu.make_async_remote_copy(
            src_ref=ids.at[0], dst_ref=ids.at[p], send_sem=ids_send, recv_sem=ids_recv.at[p],
            device_id=peer, device_id_type=MESH,
        ).start()
        pltpu.make_async_remote_copy(
            src_ref=feats.at[0], dst_ref=feats.at[p], send_sem=feat_send, recv_sem=feat_recv.at[p],
            device_id=peer, device_id_type=MESH,
        ).start()

    row_lanes = lax.broadcasted_iota(jnp.int32, (1, rows), 1)

    def gather_one(p):
        if not isinstance(p, int) or p > 0:
            pltpu.make_async_copy(ids.at[p], ids.at[p], ids_recv.at[p]).wait()
            pltpu.make_async_copy(feats.at[p], feats.at[p], feat_recv.at[p]).wait()
        mine = pltpu.roll(ids[p], devices - m, axis=1)
        pieces = []
        for target in range(graphs):
            column = mine[:, target * leaves : target * leaves + 1]
            pieces.append((column == row_lanes).astype(F32).astype(BF16))
        picked = jnp.dot(
            jnp.concatenate(pieces, axis=0), feats[p], preferred_element_type=F32
        ).astype(BF16)
        for target in range(graphs):
            outgoing[target, pl.ds(p * CAP, CAP), :] = picked[target * CAP : (target + 1) * CAP]
        inputs_t[p, 0:f_in, :] = feats[p].T

    def send_pair(first):
        @pl.loop(1, graphs)
        def _(step):
            target = lax.rem(g + step, graphs)
            part = pl.ds(first * CAP, 2 * CAP)
            pltpu.make_async_remote_copy(
                src_ref=outgoing.at[target, part],
                dst_ref=arrived.at[g, part],
                send_sem=row_send,
                recv_sem=row_recv.at[g],
                device_id=(target, m),
                device_id_type=MESH,
            ).start()

    def build_selector():
        @pl.loop(0, groups)
        def _(tg):
            base = pl.multiple_of(tg * GROUP, GROUP)
            node_ids = split_feature[pl.ds(base, GROUP), :]
            cuts = threshold[pl.ds(base, GROUP), :]
            high = cuts.astype(BF16).astype(F32)
            middle = (cuts - high).astype(BF16).astype(F32)
            low = cuts - high - middle
            for node in range(inner):
                column = jnp.broadcast_to(node_ids[:, node : node + 1], (GROUP, 128))
                parts = []
                for q in range(4):
                    parts.append(jnp.where(column == lanes + q * 128, 1.0, 0.0))
                last = parts[3]
                for extra, part in enumerate((high, middle, low)):
                    last = jnp.where(lanes == 64 + extra, -part[:, node : node + 1], last)
                parts[3] = last
                selector[tg, place[node] * GROUP : (place[node] + 1) * GROUP, :] = jnp.concatenate(
                    parts, axis=1
                ).astype(BF16)
            values = leaf_value[pl.ds(base, GROUP), :]
            for pair in range((inner + 1) // 2):
                left = values[:, 2 * pair : 2 * pair + 1]
                right = values[:, 2 * pair + 1 : 2 * pair + 2]
                where = slice(pair * GROUP, (pair + 1) * GROUP)
                scale = 1.0 / (inner + 1)
                leaf_mid[tg, where, :] = jnp.broadcast_to((left + right) * scale, (GROUP, 128))
                leaf_half[tg, where, :] = jnp.broadcast_to((right - left) * scale, (GROUP, 128))

    def build_counts():
        degrees = jnp.broadcast_to(degree[...].astype(F32), (128, rows)).T
        degree_col[...] = degrees
        for j in range(entries):
            named = jnp.broadcast_to(neighbour_slot[:, j : j + 1], (rows, 128)) ^ (m * CAP)
            slot_ids[j] = jnp.where(degrees > j + 0.5, named, -1)

        @pl.loop(0, graphs)
        def _(source):
            for half in range(width // 128):
                here = lanes + (source * width + half * 128)
                for part in range(0, rows, 128):
                    total = jnp.zeros((128, 128), F32)
                    for j in range(entries):
                        total = total + jnp.where(slot_ids[j, part : part + 128] == here, 1.0, 0.0)
                    counts[source, part : part + 128, half * 128 : (half + 1) * 128] = total.astype(
                        BF16
                    )

    def build_rest():
        own_term[...] = (
            jnp.dot(features[...], self_weight[...], preferred_element_type=F32) + hidden_bias[...]
        )
        padded = jnp.concatenate(
            [out_weight[...].astype(F32), jnp.zeros((out_weight.shape[0], 128 - emb), F32)], axis=1
        )
        out_weight_t[...] = padded.T[:emb].astype(BF16)
        for place_at, row in enumerate((out_bias, out_gain)):
            wide_row = jnp.concatenate([row[...], jnp.zeros((1, 128 - emb), F32)], axis=1)
            out_cols[place_at] = jnp.broadcast_to(wide_row, (128, 128)).T[:emb]
        for p in range(leaves):
            inputs_t[p, f_in + emb :, :] = jnp.ones((512 - f_in - emb, rows), BF16)

    pair_order = (0, 2, 6, 4) if leaves == 8 else tuple(range(0, leaves, 2))
    fillers = [build_selector, build_rest, build_counts]
    for at, first in enumerate(pair_order):
        gather_one(first)
        gather_one(first + 1)
        send_pair(first)
        if at < len(fillers):
            fillers[at]()
    for filler in fillers[len(pair_order) :]:
        filler()

    summed[...] = jnp.dot(counts[g], outgoing[g], preferred_element_type=F32)

    @pl.loop(1, graphs)
    def _(step):
        source = lax.rem(g + graphs - step, graphs)
        pltpu.make_async_copy(
            arrived.at[source], arrived.at[source], row_recv.at[source]
        ).wait()
        summed[...] += jnp.dot(counts[source], arrived[source], preferred_element_type=F32)

    by = jnp.concatenate([degree_col[...]] * (f_in // 128), axis=1)
    mean = (summed[...] / by).astype(BF16)
    hidden = jnp.maximum(
        own_term[...] + jnp.dot(mean, neigh_weight[...], preferred_element_type=F32), 0.0
    ).astype(BF16)
    across = rows // 128
    raw = lax.dot_general(
        out_weight_t[...], hidden, (((1,), (1,)), ((), ())), preferred_element_type=F32
    ) + jnp.concatenate([out_cols[0]] * across, axis=1)
    level = lax.rsqrt(jnp.sum(raw * raw, axis=0, keepdims=True) * (1.0 / emb) + NORM_EPS)
    made_t = raw * level * jnp.concatenate([out_cols[1]] * across, axis=1)
    inputs_t[0, f_in : f_in + emb, :] = made_t.astype(BF16)

    @pl.loop(1, leaves)
    def _(i):
        p = leaf_order(i)
        part = pl.ds(f_in, emb)
        pltpu.make_async_remote_copy(
            src_ref=inputs_t.at[0, part], dst_ref=inputs_t.at[p, part], send_sem=emb_send,
            recv_sem=emb_recv.at[p], device_id=(g, flip(m, p, leaves)), device_id_type=MESH,
        ).start()

    made = jnp.concatenate([made_t, jnp.zeros((128 - emb, rows), F32)], axis=0).T
    embedding[...] = made[:, :emb].astype(BF16)

    def one_group(p, tg, column):
        margin = jnp.dot(selector[tg], inputs_t[p], preferred_element_type=F32)

        def value(node, half):
            at = place[node] * GROUP
            if 2 * node + 1 >= inner:
                pair = node - inner // 2
                low = leaf_mid[tg, pair * GROUP : (pair + 1) * GROUP, :]
                gap = leaf_half[tg, pair * GROUP : (pair + 1) * GROUP, :]
            else:
                left = value(2 * node + 1, half)
                right = value(2 * node + 2, half)
                low = left + right
                gap = right - left
            turn = jnp.tanh(margin[at : at + GROUP, half * 128 : (half + 1) * 128])
            return low + turn * gap

        for half in range(rows // 128):
            total = value(0, half)
            where = slice(half * 128, (half + 1) * 128)
            partial[column, :, where] += total[:8] + total[8:]

    @pl.loop(0, leaves)
    def _(i):
        p = leaf_order(i)

        @pl.when(i > 0)
        def _():
            part = inputs_t.at[p, pl.ds(f_in, emb)]
            pltpu.make_async_copy(part, part, emb_recv.at[p]).wait()

        partial[p] = jnp.zeros(partial.shape[1:], F32)

        @pl.loop(0, groups)
        def _(tg):
            one_group(p, tg, p)

        @pl.when(i > 0)
        def _():
            pltpu.make_async_remote_copy(
                src_ref=partial.at[p], dst_ref=partial_in.at[p], send_sem=score_send,
                recv_sem=score_recv.at[p], device_id=(g, flip(m, p, leaves)), device_id_type=MESH,
            ).start()

    running = partial[0]
    for p in range(1, leaves):
        pltpu.make_async_copy(partial_in.at[p], partial_in.at[p], score_recv.at[p]).wait()
        running = running + partial_in[p]
    scores[...] = jnp.sum(running, axis=0, keepdims=True)

    others = pl.ds(0, leaves - 1)
    pltpu.make_async_copy(ids.at[others], ids.at[others], ids_send).wait()
    pltpu.make_async_copy(feats.at[others], feats.at[others], feat_send).wait()
    block = outgoing.at[pl.ds(0, graphs - 1)]
    pltpu.make_async_copy(block, block, row_send).wait()
    block = inputs_t.at[others, pl.ds(f_in, emb)]
    pltpu.make_async_copy(block, block, emb_send).wait()
    pltpu.make_async_copy(partial.at[others], partial.at[others], score_send).wait()


def on_device(
    graphs,
    leaves,
    features,
    send_rows,
    neighbour_slot,
    degree,
    self_weight,
    neigh_weight,
    hidden_bias,
    out_weight,
    out_bias,
    out_gain,
    split_feature,
    threshold,
    leaf_value,
):
    rows, f_in = features.shape
    hid = self_weight.shape[1]
    emb = out_weight.shape[1]
    trees, inner = split_feature.shape
    groups = trees // GROUP
    width = leaves * CAP
    entries = neighbour_slot.shape[1]
    dma = pltpu.SemaphoreType.DMA
    vmem = pl.BlockSpec(memory_space=pltpu.VMEM)
    embedding, scores = pl.pallas_call(
        functools.partial(kernel, graphs, leaves),
        out_shape=(
            jax.ShapeDtypeStruct((rows, emb), BF16),
            jax.ShapeDtypeStruct((1, rows), F32),
        ),
        in_specs=[vmem] * 13,
        out_specs=(vmem, vmem),
        scratch_shapes=[
            pltpu.VMEM((leaves, rows, f_in), BF16),
            pltpu.VMEM((leaves, CAP, graphs * leaves), jnp.int32),
            pltpu.VMEM((graphs, width, f_in), BF16),
            pltpu.VMEM((graphs, width, f_in), BF16),
            pltpu.VMEM((entries, rows, 128), jnp.int32),
            pltpu.VMEM((graphs, rows, width), BF16),
            pltpu.VMEM((groups, inner * GROUP, 512), BF16),
            pltpu.VMEM((groups, (inner + 1) // 2 * GROUP, 128), F32),
            pltpu.VMEM((groups, (inner + 1) // 2 * GROUP, 128), F32),
            pltpu.VMEM((leaves, 512, rows), BF16),
            pltpu.VMEM((rows, hid), F32),
            pltpu.VMEM((emb, hid), BF16),
            pltpu.VMEM((2, emb, 128), F32),
            pltpu.VMEM((rows, 128), F32),
            pltpu.VMEM((rows, f_in), F32),
            pltpu.VMEM((leaves, 8, rows), F32),
            pltpu.VMEM((leaves, 8, rows), F32),
            dma,
            dma,
            dma,
            dma,
            dma,
            dma((leaves,)),
            dma((leaves,)),
            dma((graphs,)),
            dma((leaves,)),
            dma((leaves,)),
        ],
        compiler_params=pltpu.CompilerParams(
            collective_id=0, has_side_effects=True, vmem_limit_bytes=56 * 2**20
        ),
        name="sage_forest",
    )(
        features,
        send_rows.reshape(send_rows.shape[1:]),
        neighbour_slot,
        degree.reshape(1, rows),
        self_weight,
        neigh_weight,
        hidden_bias.reshape(1, hid),
        out_weight,
        out_bias.reshape(1, emb),
        out_gain.reshape(1, emb),
        split_feature,
        threshold,
        leaf_value,
    )
    return (embedding, scores.reshape(rows))


def solution(mesh):
    in_specs = (
        P(("graph", "leaf"), None),
        P(("graph", "leaf"), None, None),
        P(("graph", "leaf"), None),
        P(("graph", "leaf")),
        P(),
        P(),
        P(),
        P(),
        P(),
        P(),
        P("leaf", None),
        P("leaf", None),
        P("leaf", None),
    )
    out_specs = (P(("graph", "leaf"), None), P(("graph", "leaf")))
    return jax.shard_map(
        functools.partial(on_device, mesh.shape["graph"], mesh.shape["leaf"]),
        mesh=mesh,
        in_specs=in_specs,
        out_specs=out_specs,
        check_vma=False,
    )
```

```python
import functools

import jax
import jax.numpy as jnp
from jax import lax
from jax.experimental import pallas as pl
from jax.experimental.pallas import tpu as pltpu
from jax.sharding import PartitionSpec as P

NORM_EPS = 1e-05
CAP = 32
GROUP = 16
BF16 = jnp.bfloat16
F32 = jnp.float32
MESH = pl.DeviceIdType.MESH


def post_order(inner):
    order = []

    def visit(node):
        if node < inner:
            visit(2 * node + 1)
            visit(2 * node + 2)
            order.append(node)

    visit(0)
    place = [0] * inner
    for position, node in enumerate(order):
        place[node] = position
    return place


def flip(a, b, size):
    total = 0
    bit = 1
    while bit < size:
        total = total + ((a // bit + b // bit) % 2) * bit
        bit *= 2
    return total


def kernel(
    graphs,
    leaves,
    features,
    send_rows,
    neighbour_slot,
    degree,
    self_weight,
    neigh_weight,
    hidden_bias,
    out_weight_t,
    out_bias,
    out_gain,
    split_feature,
    threshold,
    leaf_value,
    embedding_t,
    scores,
    feats,
    ids,
    outgoing,
    arrived,
    slot_ids,
    counts,
    selector,
    leaf_mid,
    leaf_half,
    feat_t,
    emb_t,
    margins,
    own_term,
    out_cols,
    degree_col,
    summed,
    partial,
    partial_in,
    feat_send,
    ids_send,
    row_send,
    emb_send,
    score_send,
    feat_recv,
    ids_recv,
    row_recv,
    emb_recv,
    score_recv,
):
    g = lax.axis_index("graph")
    m = lax.axis_index("leaf")
    rows, f_in = features.shape
    trees, inner = split_feature.shape
    emb = out_weight_t.shape[0]
    entries = neighbour_slot.shape[0]
    width = leaves * CAP
    groups = trees // GROUP
    place = post_order(inner)
    lanes = lax.broadcasted_iota(jnp.int32, (1, 128), 1)

    barrier = pltpu.get_barrier_semaphore()

    @pl.loop(1, graphs)
    def _(step):
        pl.semaphore_signal(
            barrier, inc=1, device_id=(lax.rem(g + step, graphs), m), device_id_type=MESH
        )

    @pl.loop(1, leaves)
    def _(step):
        pl.semaphore_signal(
            barrier, inc=1, device_id=(g, flip(m, step, leaves)), device_id_type=MESH
        )

    devices = graphs * leaves
    ids[0] = send_rows[...]
    feats[0] = features[...]

    def leaf_order(i):
        if leaves == 8:
            return i + 2 * ((i // 4) * (1 - 2 * ((i // 2) % 2)))
        return i

    def send_feats(source, p):
        pltpu.make_async_remote_copy(
            src_ref=feats.at[source],
            dst_ref=feats.at[flip(source, p, leaves)],
            send_sem=feat_send,
            recv_sem=feat_recv.at[flip(source, p, leaves)],
            device_id=(g, flip(m, p, leaves)),
            device_id_type=MESH,
        ).start()

    row_lanes = lax.broadcasted_iota(jnp.int32, (1, rows), 1)

    def gather_one(p):
        if p > 0:
            pltpu.make_async_copy(ids.at[p], ids.at[p], ids_recv.at[p]).wait()
            pltpu.make_async_copy(feats.at[p], feats.at[p], feat_recv.at[p]).wait()
            if p % 2 == 0:
                send_feats(p, 1)
        mine = pltpu.roll(ids[p], devices - m, axis=1)
        pieces = []
        for target in range(graphs):
            column = mine[:, target * leaves : target * leaves + 1]
            pieces.append((column == row_lanes).astype(F32).astype(BF16))
        picked = jnp.dot(
            jnp.concatenate(pieces, axis=0), feats[p], preferred_element_type=F32
        ).astype(BF16)
        for target in range(graphs):
            outgoing[target, pl.ds(p * CAP, CAP), :] = picked[target * CAP : (target + 1) * CAP]

    def send_part(p):
        @pl.loop(1, graphs)
        def _(step):
            target = lax.rem(g + step, graphs)
            part = pl.ds(p * CAP, CAP)
            pltpu.make_async_remote_copy(
                src_ref=outgoing.at[target, part],
                dst_ref=arrived.at[g, part],
                send_sem=row_send,
                recv_sem=row_recv.at[g],
                device_id=(target, m),
                device_id_type=MESH,
            ).start()

    def build_selector():
        @pl.loop(0, groups)
        def _(tg):
            base = pl.multiple_of(tg * GROUP, GROUP)
            node_ids = split_feature[pl.ds(base, GROUP), :]
            cuts = threshold[pl.ds(base, GROUP), :]
            high = cuts.astype(BF16).astype(F32)
            middle = (cuts - high).astype(BF16).astype(F32)
            low = cuts - high - middle
            for node in range(inner):
                column = jnp.broadcast_to(node_ids[:, node : node + 1], (GROUP, 128))
                parts = []
                for q in range(4):
                    parts.append(jnp.where(column == lanes + q * 128, 1.0, 0.0))
                last = parts[3]
                for extra, part in enumerate((high, middle, low)):
                    last = jnp.where(lanes == 64 + extra, -part[:, node : node + 1], last)
                parts[3] = last
                selector[tg, place[node] * GROUP : (place[node] + 1) * GROUP, :] = jnp.concatenate(
                    parts, axis=1
                ).astype(BF16)
            values = leaf_value[pl.ds(base, GROUP), :]
            for pair in range((inner + 1) // 2):
                left = values[:, 2 * pair : 2 * pair + 1]
                right = values[:, 2 * pair + 1 : 2 * pair + 2]
                where = slice(pair * GROUP, (pair + 1) * GROUP)
                scale = 1.0 / (inner + 1)
                leaf_mid[tg, where, :] = jnp.broadcast_to((left + right) * scale, (GROUP, 128))
                leaf_half[tg, where, :] = jnp.broadcast_to((right - left) * scale, (GROUP, 128))

    def build_counts():
        degrees = jnp.broadcast_to(degree[...].astype(F32), (128, rows)).T
        degree_col[...] = degrees
        named_all = jnp.concatenate(
            [neighbour_slot[...], jnp.zeros((128 - entries, rows), jnp.int32)], axis=0
        ).T ^ (m * CAP)
        for j in range(entries):
            named = jnp.broadcast_to(named_all[:, j : j + 1], (rows, 128))
            slot_ids[j] = jnp.where(degrees > j + 0.5, named, -1)

        @pl.loop(0, graphs)
        def _(source):
            for half in range(width // 128):
                here = lanes + (source * width + half * 128)
                for part in range(0, rows, 128):
                    total = jnp.zeros((128, 128), F32)
                    for j in range(entries):
                        total = total + jnp.where(slot_ids[j, part : part + 128] == here, 1.0, 0.0)
                    counts[source, part : part + 128, half * 128 : (half + 1) * 128] = total.astype(
                        BF16
                    )

    def build_rest():
        own_term[...] = (
            jnp.dot(features[...], self_weight[...], preferred_element_type=F32) + hidden_bias[...]
        )
        for place_at, row in enumerate((out_bias, out_gain)):
            wide_row = jnp.concatenate([row[...], jnp.zeros((1, 128 - emb), F32)], axis=1)
            out_cols[place_at] = jnp.broadcast_to(wide_row, (128, 128)).T[:emb]
        for pair in range(leaves // 2):
            emb_t[pair, emb:, :] = jnp.ones((128 - emb, 2 * rows), BF16)

    def build_margins():
        @pl.loop(0, leaves // 2)
        def _(pair):
            for core in range(2):
                feat_t[:, core * rows : (core + 1) * rows] = feats[2 * pair + core].T

            @pl.loop(0, groups)
            def _(tg):
                margins[pair, tg] = jnp.dot(
                    selector[tg, :, :f_in], feat_t[...], preferred_element_type=F32
                )

    pair_order = (0, 2, 6, 4) if leaves == 8 else tuple(range(0, leaves, 2))
    gather_one(0)
    pl.semaphore_wait(barrier, graphs - 1 + leaves - 1)

    @pl.loop(1, leaves)
    def _(i):
        p = leaf_order(i)
        pltpu.make_async_remote_copy(
            src_ref=ids.at[0], dst_ref=ids.at[p], send_sem=ids_send, recv_sem=ids_recv.at[p],
            device_id=(g, flip(m, p, leaves)), device_id_type=MESH,
        ).start()

    for p in (1,) + pair_order[1:]:
        send_feats(0, p)
    send_part(0)
    gather_one(1)
    send_part(1)
    build_selector()
    for at, first in enumerate(pair_order[1:]):
        for p in (first, first + 1):
            gather_one(p)
            send_part(p)
        if at == 0:
            build_rest()
    build_counts()
    build_margins()

    summed[...] = jnp.dot(counts[g], outgoing[g], preferred_element_type=F32)

    @pl.loop(1, graphs)
    def _(step):
        source = lax.rem(g + graphs - step, graphs)
        pltpu.make_async_copy(arrived.at[source], arrived.at[source], row_recv.at[source]).wait()
        summed[...] += jnp.dot(counts[source], arrived[source], preferred_element_type=F32)

    by = jnp.concatenate([degree_col[...]] * (f_in // 128), axis=1)
    mean = (summed[...] / by).astype(BF16)
    hidden = jnp.maximum(
        own_term[...] + jnp.dot(mean, neigh_weight[...], preferred_element_type=F32), 0.0
    ).astype(BF16)
    across = rows // 128
    raw = lax.dot_general(
        out_weight_t[...], hidden, (((1,), (1,)), ((), ())), preferred_element_type=F32
    ) + jnp.concatenate([out_cols[0]] * across, axis=1)
    level = lax.rsqrt(jnp.sum(raw * raw, axis=0, keepdims=True) * (1.0 / emb) + NORM_EPS)
    made_t = raw * level * jnp.concatenate([out_cols[1]] * across, axis=1)
    embedded_t = made_t.astype(BF16)
    emb_t[0, 0:emb, 0:rows] = embedded_t

    def emb_slot(p):
        return emb_t.at[p // 2, pl.ds(0, emb), pl.ds(pl.multiple_of(p % 2 * rows, rows), rows)]

    @pl.loop(1, leaves)
    def _(i):
        p = leaf_order(i)
        pltpu.make_async_remote_copy(
            src_ref=emb_slot(0), dst_ref=emb_slot(p), send_sem=emb_send.at[p],
            recv_sem=emb_recv.at[p], device_id=(g, flip(m, p, leaves)), device_id_type=MESH,
        ).start()

    embedding_t[...] = embedded_t

    def one_group(pair, tg):
        late = jnp.dot(selector[tg, :, f_in:], emb_t[pair], preferred_element_type=F32)

        def value(node, part):
            at = place[node] * GROUP
            if 2 * node + 1 >= inner:
                leaf = node - inner // 2
                low = leaf_mid[tg, leaf * GROUP : (leaf + 1) * GROUP, :]
                gap = leaf_half[tg, leaf * GROUP : (leaf + 1) * GROUP, :]
            else:
                left = value(2 * node + 1, part)
                right = value(2 * node + 2, part)
                low = left + right
                gap = right - left
            where = slice(part * 128, (part + 1) * 128)
            turn = jnp.tanh(
                margins[pair, tg, at : at + GROUP, where] + late[at : at + GROUP, where]
            )
            return low + turn * gap

        for core in range(2):
            for part in range(rows // 128):
                total = value(0, core * (rows // 128) + part)
                where = slice(part * 128, (part + 1) * 128)
                partial[2 * pair + core, :, where] += total[:8] + total[8:]

    def arrive(p):
        pltpu.make_async_copy(emb_slot(p), emb_slot(p), emb_recv.at[p]).wait()

    def leave(p):
        pltpu.make_async_remote_copy(
            src_ref=partial.at[p], dst_ref=partial_in.at[p], send_sem=score_send,
            recv_sem=score_recv.at[p], device_id=(g, flip(m, p, leaves)), device_id_type=MESH,
        ).start()

    partial[...] = jnp.zeros(partial.shape, F32)
    arrive(1)
    early = groups // 2

    @pl.loop(0, leaves // 2 * groups)
    def _(step):
        at = step + groups - early
        turn = at // groups % (leaves // 2)
        tg = at % groups
        pair = leaf_order(2 * turn) // 2

        @pl.when(jnp.logical_and(turn > 0, tg == 0))
        def _():
            arrive(2 * pair)
            arrive(2 * pair + 1)

        one_group(pair, tg)

        @pl.when(jnp.logical_and(turn > 0, tg == groups - 1))
        def _():
            leave(2 * pair)
            leave(2 * pair + 1)

    leave(1)
    running = partial[0]
    for p in range(1, leaves):
        pltpu.make_async_copy(partial_in.at[p], partial_in.at[p], score_recv.at[p]).wait()
        running = running + partial_in[p]
    scores[...] = jnp.sum(running, axis=0, keepdims=True)

    others = pl.ds(0, leaves - 1)
    pltpu.make_async_copy(ids.at[others], ids.at[others], ids_send).wait()
    pltpu.make_async_copy(feats.at[others], feats.at[others], feat_send).wait()
    block = outgoing.at[pl.ds(0, graphs - 1)]
    pltpu.make_async_copy(block, block, row_send).wait()
    for p in range(1, leaves):
        pltpu.make_async_copy(emb_slot(p), emb_slot(p), emb_send.at[p]).wait()
    pltpu.make_async_copy(partial.at[others], partial.at[others], score_send).wait()


def on_device(
    graphs,
    leaves,
    features,
    send_rows,
    neighbour_slot,
    degree,
    self_weight,
    neigh_weight,
    hidden_bias,
    out_weight,
    out_bias,
    out_gain,
    split_feature,
    threshold,
    leaf_value,
):
    rows, f_in = features.shape
    hid = self_weight.shape[1]
    emb = out_weight.shape[1]
    trees, inner = split_feature.shape
    groups = trees // GROUP
    width = leaves * CAP
    entries = neighbour_slot.shape[1]
    dma = pltpu.SemaphoreType.DMA
    vmem = pl.BlockSpec(memory_space=pltpu.VMEM)
    embedding_t, scores = pl.pallas_call(
        functools.partial(kernel, graphs, leaves),
        out_shape=(
            jax.ShapeDtypeStruct((emb, rows), BF16),
            jax.ShapeDtypeStruct((1, rows), F32),
        ),
        in_specs=[vmem] * 13,
        out_specs=(vmem, vmem),
        scratch_shapes=[
            pltpu.VMEM((leaves, rows, f_in), BF16),
            pltpu.VMEM((leaves, CAP, graphs * leaves), jnp.int32),
            pltpu.VMEM((graphs, width, f_in), BF16),
            pltpu.VMEM((graphs, width, f_in), BF16),
            pltpu.VMEM((entries, rows, 128), jnp.int32),
            pltpu.VMEM((graphs, rows, width), BF16),
            pltpu.VMEM((groups, inner * GROUP, 512), BF16),
            pltpu.VMEM((groups, (inner + 1) // 2 * GROUP, 128), F32),
            pltpu.VMEM((groups, (inner + 1) // 2 * GROUP, 128), F32),
            pltpu.VMEM((f_in, 2 * rows), BF16),
            pltpu.VMEM((leaves // 2, 128, 2 * rows), BF16),
            pltpu.VMEM((leaves // 2, groups, inner * GROUP, 2 * rows), F32),
            pltpu.VMEM((rows, hid), F32),
            pltpu.VMEM((2, emb, 128), F32),
            pltpu.VMEM((rows, 128), F32),
            pltpu.VMEM((rows, f_in), F32),
            pltpu.VMEM((leaves, 8, rows), F32),
            pltpu.VMEM((leaves, 8, rows), F32),
            dma,
            dma,
            dma,
            dma((leaves,)),
            dma,
            dma((leaves,)),
            dma((leaves,)),
            dma((graphs,)),
            dma((leaves,)),
            dma((leaves,)),
        ],
        compiler_params=pltpu.CompilerParams(
            collective_id=0, has_side_effects=True, vmem_limit_bytes=62 * 2**20
        ),
        name="sage_forest",
    )(
        features,
        send_rows.reshape(send_rows.shape[1:]).T,
        neighbour_slot.T,
        degree.reshape(1, rows),
        self_weight,
        neigh_weight,
        hidden_bias.reshape(1, hid),
        out_weight.T,
        out_bias.reshape(1, emb),
        out_gain.reshape(1, emb),
        split_feature,
        threshold,
        leaf_value,
    )
    return (embedding_t.T, scores.reshape(rows))


def solution(mesh):
    in_specs = (
        P(("graph", "leaf"), None),
        P(("graph", "leaf"), None, None),
        P(("graph", "leaf"), None),
        P(("graph", "leaf")),
        P(),
        P(),
        P(),
        P(),
        P(),
        P(),
        P("leaf", None),
        P("leaf", None),
        P("leaf", None),
    )
    out_specs = (P(("graph", "leaf"), None), P(("graph", "leaf")))
    return jax.shard_map(
        functools.partial(on_device, mesh.shape["graph"], mesh.shape["leaf"]),
        mesh=mesh,
        in_specs=in_specs,
        out_specs=out_specs,
        check_vma=False,
    )
```

```python
import functools

import jax
import jax.numpy as jnp
from jax import lax
from jax.experimental import pallas as pl
from jax.experimental.pallas import tpu as pltpu
from jax.sharding import PartitionSpec as P

NORM_EPS = 1e-05
CAP = 32
GROUP = 16
BF16 = jnp.bfloat16
F32 = jnp.float32
MESH = pl.DeviceIdType.MESH


def post_order(inner):
    order = []

    def visit(node):
        if node < inner:
            visit(2 * node + 1)
            visit(2 * node + 2)
            order.append(node)

    visit(0)
    place = [0] * inner
    for position, node in enumerate(order):
        place[node] = position
    return place


def flip(a, b, size):
    total = 0
    bit = 1
    while bit < size:
        total = total + ((a // bit + b // bit) % 2) * bit
        bit *= 2
    return total


def kernel(
    graphs,
    leaves,
    features,
    send_rows,
    neighbour_slot,
    degree,
    self_weight,
    neigh_weight,
    hidden_bias,
    out_weight_t,
    out_bias,
    out_gain,
    split_feature,
    threshold,
    leaf_value,
    embedding_t,
    scores,
    feats,
    ids,
    outgoing,
    arrived,
    slot_ids,
    counts,
    selector,
    leaf_mid,
    leaf_half,
    feat_t,
    emb_t,
    margins,
    own_term,
    out_cols,
    degree_col,
    summed,
    partial,
    partial_in,
    feat_send,
    ids_send,
    row_send,
    emb_send,
    score_send,
    feat_recv,
    ids_recv,
    row_recv,
    emb_recv,
    score_recv,
):
    g = lax.axis_index("graph")
    m = lax.axis_index("leaf")
    rows, f_in = features.shape
    trees, inner = split_feature.shape
    emb = out_weight_t.shape[0]
    entries = neighbour_slot.shape[0]
    width = leaves * CAP
    groups = trees // GROUP
    place = post_order(inner)
    lanes = lax.broadcasted_iota(jnp.int32, (1, 128), 1)

    barrier = pltpu.get_barrier_semaphore()

    @pl.loop(1, graphs)
    def _(step):
        pl.semaphore_signal(
            barrier, inc=1, device_id=(lax.rem(g + step, graphs), m), device_id_type=MESH
        )

    @pl.loop(1, leaves)
    def _(step):
        pl.semaphore_signal(
            barrier, inc=1, device_id=(g, flip(m, step, leaves)), device_id_type=MESH
        )

    devices = graphs * leaves
    ids[0] = send_rows[...]
    feats[0] = features[...]

    def leaf_order(i):
        if leaves == 8:
            return i + 2 * ((i // 4) * (1 - 2 * ((i // 2) % 2)))
        return i

    def send_feats(source, p):
        pltpu.make_async_remote_copy(
            src_ref=feats.at[source],
            dst_ref=feats.at[flip(source, p, leaves)],
            send_sem=feat_send,
            recv_sem=feat_recv.at[flip(source, p, leaves)],
            device_id=(g, flip(m, p, leaves)),
            device_id_type=MESH,
        ).start()

    row_lanes = lax.broadcasted_iota(jnp.int32, (1, rows), 1)

    def gather_one(p):
        if p > 0:
            pltpu.make_async_copy(ids.at[p], ids.at[p], ids_recv.at[p]).wait()
            pltpu.make_async_copy(feats.at[p], feats.at[p], feat_recv.at[p]).wait()
            if p % 2 == 0:
                send_feats(p, 1)
        mine = pltpu.roll(ids[p], devices - m, axis=1)
        pieces = []
        for target in range(graphs):
            column = mine[:, target * leaves : target * leaves + 1]
            pieces.append((column == row_lanes).astype(F32).astype(BF16))
        picked = jnp.dot(
            jnp.concatenate(pieces, axis=0), feats[p], preferred_element_type=F32
        ).astype(BF16)
        for target in range(graphs):
            outgoing[target, pl.ds(p * CAP, CAP), :] = picked[target * CAP : (target + 1) * CAP]

    def send_part(p):
        @pl.loop(1, graphs)
        def _(step):
            target = lax.rem(g + step, graphs)
            part = pl.ds(p * CAP, CAP)
            pltpu.make_async_remote_copy(
                src_ref=outgoing.at[target, part],
                dst_ref=arrived.at[g, part],
                send_sem=row_send,
                recv_sem=row_recv.at[g],
                device_id=(target, m),
                device_id_type=MESH,
            ).start()

    def build_selector():
        @pl.loop(0, groups)
        def _(tg):
            base = pl.multiple_of(tg * GROUP, GROUP)
            node_ids = split_feature[pl.ds(base, GROUP), :]
            cuts = threshold[pl.ds(base, GROUP), :]
            high = cuts.astype(BF16).astype(F32)
            middle = (cuts - high).astype(BF16).astype(F32)
            low = cuts - high - middle
            for node in range(inner):
                column = jnp.broadcast_to(node_ids[:, node : node + 1], (GROUP, 128))
                parts = []
                for q in range(4):
                    parts.append(jnp.where(column == lanes + q * 128, 1.0, 0.0))
                last = parts[3]
                for extra, part in enumerate((high, middle, low)):
                    last = jnp.where(lanes == 64 + extra, -part[:, node : node + 1], last)
                parts[3] = last
                selector[tg, place[node] * GROUP : (place[node] + 1) * GROUP, :] = jnp.concatenate(
                    parts, axis=1
                ).astype(BF16)
            values = leaf_value[pl.ds(base, GROUP), :]
            for pair in range((inner + 1) // 2):
                left = values[:, 2 * pair : 2 * pair + 1]
                right = values[:, 2 * pair + 1 : 2 * pair + 2]
                where = slice(pair * GROUP, (pair + 1) * GROUP)
                scale = 1.0 / (inner + 1)
                leaf_mid[tg, where, :] = jnp.broadcast_to((left + right) * scale, (GROUP, 128))
                leaf_half[tg, where, :] = jnp.broadcast_to((right - left) * scale, (GROUP, 128))

    def build_counts():
        degrees = jnp.broadcast_to(degree[...].astype(F32), (128, rows)).T
        degree_col[...] = degrees
        named_all = jnp.concatenate(
            [neighbour_slot[...], jnp.zeros((128 - entries, rows), jnp.int32)], axis=0
        ).T ^ (m * CAP)
        for j in range(entries):
            named = jnp.broadcast_to(named_all[:, j : j + 1], (rows, 128))
            slot_ids[j] = jnp.where(degrees > j + 0.5, named, -1)

        @pl.loop(0, graphs)
        def _(source):
            for half in range(width // 128):
                here = lanes + (source * width + half * 128)
                for part in range(0, rows, 128):
                    total = jnp.zeros((128, 128), F32)
                    for j in range(entries):
                        total = total + jnp.where(slot_ids[j, part : part + 128] == here, 1.0, 0.0)
                    counts[source, part : part + 128, half * 128 : (half + 1) * 128] = total.astype(
                        BF16
                    )

    def build_rest():
        own_term[...] = (
            jnp.dot(features[...], self_weight[...], preferred_element_type=F32) + hidden_bias[...]
        )
        for place_at, row in enumerate((out_bias, out_gain)):
            wide_row = jnp.concatenate([row[...], jnp.zeros((1, 128 - emb), F32)], axis=1)
            out_cols[place_at] = jnp.broadcast_to(wide_row, (128, 128)).T[:emb]
        for pair in range(leaves // 2):
            emb_t[pair, emb:, :] = jnp.ones((128 - emb, 2 * rows), BF16)

    def build_margins():
        @pl.loop(0, leaves // 2)
        def _(pair):
            for core in range(2):
                feat_t[:, core * rows : (core + 1) * rows] = feats[2 * pair + core].T

            @pl.loop(0, groups)
            def _(tg):
                margins[pair, tg] = jnp.dot(
                    selector[tg, :, :f_in], feat_t[...], preferred_element_type=F32
                )

    pair_order = (0, 2, 6, 4) if leaves == 8 else tuple(range(0, leaves, 2))
    gather_one(0)
    pl.semaphore_wait(barrier, graphs - 1 + leaves - 1)

    def send_ids(p):
        pltpu.make_async_remote_copy(
            src_ref=ids.at[0], dst_ref=ids.at[p], send_sem=ids_send, recv_sem=ids_recv.at[p],
            device_id=(g, flip(m, p, leaves)), device_id_type=MESH,
        ).start()

    send_ids(1)
    send_feats(0, 1)
    send_part(0)

    @pl.loop(2, leaves)
    def _(i):
        send_ids(leaf_order(i))

    for p in pair_order[1:]:
        send_feats(0, p)
    gather_one(1)
    send_part(1)
    build_selector()
    for at, first in enumerate(pair_order[1:]):
        for p in (first, first + 1):
            gather_one(p)
            send_part(p)
        if at == 0:
            build_rest()
    build_counts()
    build_margins()

    summed[...] = jnp.dot(counts[g], outgoing[g], preferred_element_type=F32)

    @pl.loop(1, graphs)
    def _(step):
        source = lax.rem(g + graphs - step, graphs)
        pltpu.make_async_copy(arrived.at[source], arrived.at[source], row_recv.at[source]).wait()
        summed[...] += jnp.dot(counts[source], arrived[source], preferred_element_type=F32)

    by = jnp.concatenate([degree_col[...]] * (f_in // 128), axis=1)
    mean = (summed[...] / by).astype(BF16)
    hidden = jnp.maximum(
        own_term[...] + jnp.dot(mean, neigh_weight[...], preferred_element_type=F32), 0.0
    ).astype(BF16)
    across = rows // 128
    raw = lax.dot_general(
        out_weight_t[...], hidden, (((1,), (1,)), ((), ())), preferred_element_type=F32
    ) + jnp.concatenate([out_cols[0]] * across, axis=1)
    level = lax.rsqrt(jnp.sum(raw * raw, axis=0, keepdims=True) * (1.0 / emb) + NORM_EPS)
    made_t = raw * level * jnp.concatenate([out_cols[1]] * across, axis=1)
    embedded_t = made_t.astype(BF16)
    emb_t[0, 0:emb, 0:rows] = embedded_t

    def emb_slot(p):
        return emb_t.at[p // 2, pl.ds(0, emb), pl.ds(pl.multiple_of(p % 2 * rows, rows), rows)]

    @pl.loop(1, leaves)
    def _(i):
        p = leaf_order(i)
        pltpu.make_async_remote_copy(
            src_ref=emb_slot(0), dst_ref=emb_slot(p), send_sem=emb_send.at[p],
            recv_sem=emb_recv.at[p], device_id=(g, flip(m, p, leaves)), device_id_type=MESH,
        ).start()

    embedding_t[...] = embedded_t

    def one_group(pair, tg):
        late = jnp.dot(selector[tg, :, f_in:], emb_t[pair], preferred_element_type=F32)

        def value(node, part):
            at = place[node] * GROUP
            if 2 * node + 1 >= inner:
                leaf = node - inner // 2
                low = leaf_mid[tg, leaf * GROUP : (leaf + 1) * GROUP, :]
                gap = leaf_half[tg, leaf * GROUP : (leaf + 1) * GROUP, :]
            else:
                left = value(2 * node + 1, part)
                right = value(2 * node + 2, part)
                low = left + right
                gap = right - left
            where = slice(part * 128, (part + 1) * 128)
            turn = jnp.tanh(
                margins[pair, tg, at : at + GROUP, where] + late[at : at + GROUP, where]
            )
            return low + turn * gap

        for core in range(2):
            for part in range(rows // 128):
                total = value(0, core * (rows // 128) + part)
                where = slice(part * 128, (part + 1) * 128)
                partial[2 * pair + core, :, where] += total[:8] + total[8:]

    def arrive(p):
        pltpu.make_async_copy(emb_slot(p), emb_slot(p), emb_recv.at[p]).wait()

    def leave(p):
        pltpu.make_async_remote_copy(
            src_ref=partial.at[p], dst_ref=partial_in.at[p], send_sem=score_send,
            recv_sem=score_recv.at[p], device_id=(g, flip(m, p, leaves)), device_id_type=MESH,
        ).start()

    partial[...] = jnp.zeros(partial.shape, F32)

    @pl.loop(0, leaves // 2)
    def _(i):
        pair = leaf_order(2 * i) // 2

        @pl.when(i > 0)
        def _():
            arrive(2 * pair)

        arrive(2 * pair + 1)
        for tg in range(groups):
            one_group(pair, tg)

        @pl.when(i > 0)
        def _():
            leave(2 * pair)

        leave(2 * pair + 1)

    running = partial[0]
    for p in range(1, leaves):
        pltpu.make_async_copy(partial_in.at[p], partial_in.at[p], score_recv.at[p]).wait()
        running = running + partial_in[p]
    scores[...] = jnp.sum(running, axis=0, keepdims=True)

    others = pl.ds(0, leaves - 1)
    pltpu.make_async_copy(ids.at[others], ids.at[others], ids_send).wait()
    pltpu.make_async_copy(feats.at[others], feats.at[others], feat_send).wait()
    block = outgoing.at[pl.ds(0, graphs - 1)]
    pltpu.make_async_copy(block, block, row_send).wait()
    for p in range(1, leaves):
        pltpu.make_async_copy(emb_slot(p), emb_slot(p), emb_send.at[p]).wait()
    pltpu.make_async_copy(partial.at[others], partial.at[others], score_send).wait()


def on_device(
    graphs,
    leaves,
    features,
    send_rows,
    neighbour_slot,
    degree,
    self_weight,
    neigh_weight,
    hidden_bias,
    out_weight,
    out_bias,
    out_gain,
    split_feature,
    threshold,
    leaf_value,
):
    rows, f_in = features.shape
    hid = self_weight.shape[1]
    emb = out_weight.shape[1]
    trees, inner = split_feature.shape
    groups = trees // GROUP
    width = leaves * CAP
    entries = neighbour_slot.shape[1]
    dma = pltpu.SemaphoreType.DMA
    vmem = pl.BlockSpec(memory_space=pltpu.VMEM)
    embedding_t, scores = pl.pallas_call(
        functools.partial(kernel, graphs, leaves),
        out_shape=(
            pltpu.VMEM((emb, rows), BF16),
            pltpu.VMEM((1, rows), F32),
        ),
        in_specs=[vmem] * 13,
        out_specs=(vmem, vmem),
        scratch_shapes=[
            pltpu.VMEM((leaves, rows, f_in), BF16),
            pltpu.VMEM((leaves, CAP, graphs * leaves), jnp.int32),
            pltpu.VMEM((graphs, width, f_in), BF16),
            pltpu.VMEM((graphs, width, f_in), BF16),
            pltpu.VMEM((entries, rows, 128), jnp.int32),
            pltpu.VMEM((graphs, rows, width), BF16),
            pltpu.VMEM((groups, inner * GROUP, 512), BF16),
            pltpu.VMEM((groups, (inner + 1) // 2 * GROUP, 128), F32),
            pltpu.VMEM((groups, (inner + 1) // 2 * GROUP, 128), F32),
            pltpu.VMEM((f_in, 2 * rows), BF16),
            pltpu.VMEM((leaves // 2, 128, 2 * rows), BF16),
            pltpu.VMEM((leaves // 2, groups, inner * GROUP, 2 * rows), F32),
            pltpu.VMEM((rows, hid), F32),
            pltpu.VMEM((2, emb, 128), F32),
            pltpu.VMEM((rows, 128), F32),
            pltpu.VMEM((rows, f_in), F32),
            pltpu.VMEM((leaves, 8, rows), F32),
            pltpu.VMEM((leaves, 8, rows), F32),
            dma,
            dma,
            dma,
            dma((leaves,)),
            dma,
            dma((leaves,)),
            dma((leaves,)),
            dma((graphs,)),
            dma((leaves,)),
            dma((leaves,)),
        ],
        compiler_params=pltpu.CompilerParams(
            collective_id=0, has_side_effects=True, vmem_limit_bytes=62 * 2**20
        ),
        name="sage_forest",
    )(
        features,
        send_rows.reshape(send_rows.shape[1:]).T,
        neighbour_slot.T,
        degree.reshape(1, rows),
        self_weight,
        neigh_weight,
        hidden_bias.reshape(1, hid),
        out_weight.T,
        out_bias.reshape(1, emb),
        out_gain.reshape(1, emb),
        split_feature,
        threshold,
        leaf_value,
    )
    return (embedding_t.T, scores.reshape(rows))


def solution(mesh):
    in_specs = (
        P(("graph", "leaf"), None),
        P(("graph", "leaf"), None, None),
        P(("graph", "leaf"), None),
        P(("graph", "leaf")),
        P(),
        P(),
        P(),
        P(),
        P(),
        P(),
        P("leaf", None),
        P("leaf", None),
        P("leaf", None),
    )
    out_specs = (P(("graph", "leaf"), None), P(("graph", "leaf")))
    return jax.shard_map(
        functools.partial(on_device, mesh.shape["graph"], mesh.shape["leaf"]),
        mesh=mesh,
        in_specs=in_specs,
        out_specs=out_specs,
        check_vma=False,
    )
```

```python
import functools

import jax
import jax.numpy as jnp
from jax import lax
from jax.experimental import pallas as pl
from jax.experimental.pallas import tpu as pltpu
from jax.sharding import PartitionSpec as P

NORM_EPS = 1e-05
CAP = 32
GROUP = 16
SIDE = 4
EARLY = 256
BF16 = jnp.bfloat16
F32 = jnp.float32
MESH = pl.DeviceIdType.MESH


def post_order(inner):
    order = []

    def visit(node):
        if node < inner:
            visit(2 * node + 1)
            visit(2 * node + 2)
            order.append(node)

    visit(0)
    place = [0] * inner
    for position, node in enumerate(order):
        place[node] = position
    return place


def flip(a, b, size):
    total = 0
    bit = 1
    while bit < size:
        total = total + ((a // bit + b // bit) % 2) * bit
        bit *= 2
    return total


def kernel(
    graphs,
    leaves,
    features,
    send_rows,
    neighbour_slot,
    degree,
    self_weight,
    neigh_weight,
    hidden_bias,
    out_weight_t,
    out_bias,
    out_gain,
    split_feature,
    threshold,
    leaf_value,
    embedding_t,
    scores,
    feats,
    ids,
    outgoing,
    far,
    arrived,
    slot_ids,
    counts,
    selector,
    leaf_mid,
    leaf_half,
    feat_t,
    emb_t,
    margins,
    own_term,
    out_cols,
    degree_col,
    summed,
    partial,
    partial_in,
    feat_send,
    ids_send,
    row_send,
    far_send,
    emb_send,
    score_send,
    feat_recv,
    ids_recv,
    row_recv,
    emb_recv,
    score_recv,
):
    g = lax.axis_index("graph")
    m = lax.axis_index("leaf")
    rows, f_in = features.shape
    trees, inner = split_feature.shape
    emb = out_weight_t.shape[0]
    entries = neighbour_slot.shape[0]
    width = leaves * CAP
    groups = trees // GROUP
    place = post_order(inner)
    late_at = f_in - EARLY
    lanes = lax.broadcasted_iota(jnp.int32, (1, 128), 1)

    barrier = pltpu.get_barrier_semaphore()

    x, z = g // SIDE, g % SIDE

    def spot(dx, dz):
        return (x + dx) % SIDE * SIDE + (z + dz) % SIDE

    def near(i):
        return i + i // 2

    def greet(graph, leaf):
        pl.semaphore_signal(barrier, inc=1, device_id=(graph, leaf), device_id_type=MESH)

    @pl.loop(1, SIDE * leaves)
    def _(i):
        greet(spot(0, i // leaves), flip(m, i % leaves, leaves))

    @pl.loop(0, 2 * leaves)
    def _(i):
        greet(spot(1 + 2 * (i // leaves), 0), flip(m, i % leaves, leaves))

    for dx, dz in ((2, 0), (1, 1), (1, 3), (3, 1), (3, 3)):
        greet(spot(dx, dz), m)
    greeted = SIDE * leaves - 1 + 2 * leaves + 5

    devices = graphs * leaves
    ids[0] = send_rows[...]
    feats[0] = features[...]

    def leaf_order(i):
        if leaves == 8:
            return i + 2 * ((i // 4) * (1 - 2 * ((i // 2) % 2)))
        return i

    def send_feats(source, p):
        pltpu.make_async_remote_copy(
            src_ref=feats.at[source],
            dst_ref=feats.at[flip(source, p, leaves)],
            send_sem=feat_send,
            recv_sem=feat_recv.at[flip(source, p, leaves)],
            device_id=(g, flip(m, p, leaves)),
            device_id_type=MESH,
        ).start()

    row_lanes = lax.broadcasted_iota(jnp.int32, (1, rows), 1)

    def gather_one(p):
        if p > 0:
            pltpu.make_async_copy(ids.at[p], ids.at[p], ids_recv.at[p]).wait()
            pltpu.make_async_copy(feats.at[p], feats.at[p], feat_recv.at[p]).wait()
            if p % 2 == 0:
                send_feats(p, 1)
        mine = pltpu.roll(ids[p], devices - m, axis=1)
        picked = pick(mine, range(0, devices, leaves), p)
        for target in range(graphs):
            outgoing[target, pl.ds(p * CAP, CAP), :] = picked[target * CAP : (target + 1) * CAP]

    def pick(mine, columns, slot):
        pieces = []
        for column in columns:
            pieces.append((mine[:, column : column + 1] == row_lanes).astype(F32).astype(BF16))
        return jnp.dot(
            jnp.concatenate(pieces, axis=0), feats[slot], preferred_element_type=F32
        ).astype(BF16)

    def send_part(p):
        @pl.loop(1, 9)
        def _(i):
            target = spot(near(i // 3), near(i % 3))
            part = pl.ds(p * CAP, CAP)
            pltpu.make_async_remote_copy(
                src_ref=outgoing.at[target, part],
                dst_ref=arrived.at[g, part],
                send_sem=row_send,
                recv_sem=row_recv.at[g],
                device_id=(target, m),
                device_id_type=MESH,
            ).start()

    opposite = (spot(2, 0), spot(0, 2))

    def send_far_feats(axis):
        slot = leaves + axis
        for ref, send_sem, recv_sem in ((ids, ids_send, ids_recv), (feats, feat_send, feat_recv)):
            pltpu.make_async_remote_copy(
                src_ref=ref.at[0], dst_ref=ref.at[slot], send_sem=send_sem,
                recv_sem=recv_sem.at[slot], device_id=(opposite[axis], m), device_id_type=MESH,
            ).start()

    def gather_far(axis):
        slot = leaves + axis
        pltpu.make_async_copy(ids.at[slot], ids.at[slot], ids_recv.at[slot]).wait()
        pltpu.make_async_copy(feats.at[slot], feats.at[slot], feat_recv.at[slot]).wait()
        if axis == 0:
            mine = pltpu.roll(ids[slot], devices - x * (SIDE * leaves), axis=1)
            stride = leaves
        else:
            mine = pltpu.roll(ids[slot], devices - z * leaves, axis=1)
            stride = SIDE * leaves
        for half in range(2):
            columns = []
            for other in range(2 * half, 2 * half + 2):
                columns.extend(range(other * stride, other * stride + leaves))
            picked = pick(mine, columns, slot)
            for i in range(2 * leaves):
                far[axis, 2 * leaves * half + i] = picked[i * CAP : (i + 1) * CAP]

    def send_far(axis):
        source = opposite[axis]

        def piece(i):
            turn, p = i // leaves, i % leaves
            if axis == 0:
                graph, other = spot(0, turn), (z + turn) % SIDE
            else:
                graph, other = spot(near(turn), 0), (x + near(turn)) % SIDE
            leaf = flip(m, p, leaves)
            part = pl.ds(p * CAP, CAP)
            return far.at[axis, other * leaves + leaf], arrived.at[source, part], graph, leaf

        here, there, _, _ = piece(0)
        pltpu.make_async_copy(here, there, row_recv.at[source]).start()

        @pl.loop(1, (SIDE - axis) * leaves)
        def _(i):
            src, dst, graph, leaf = piece(i)
            pltpu.make_async_remote_copy(
                src_ref=src, dst_ref=dst, send_sem=far_send.at[axis],
                recv_sem=row_recv.at[source], device_id=(graph, leaf), device_id_type=MESH,
            ).start()

    def build_selector():
        @pl.loop(0, groups)
        def _(tg):
            base = pl.multiple_of(tg * GROUP, GROUP)
            node_ids = split_feature[pl.ds(base, GROUP), :]
            cuts = threshold[pl.ds(base, GROUP), :]
            high = cuts.astype(BF16).astype(F32)
            middle = (cuts - high).astype(BF16).astype(F32)
            low = cuts - high - middle
            for node in range(inner):
                column = jnp.broadcast_to(node_ids[:, node : node + 1], (GROUP, 128))
                parts = []
                for q in range(4):
                    parts.append(jnp.where(column == lanes + q * 128, 1.0, 0.0))
                last = parts[3]
                for extra, part in enumerate((high, middle, low)):
                    last = jnp.where(lanes == 64 + extra, -part[:, node : node + 1], last)
                parts[3] = last
                selector[tg, place[node] * GROUP : (place[node] + 1) * GROUP, :] = jnp.concatenate(
                    parts, axis=1
                ).astype(BF16)
            values = leaf_value[pl.ds(base, GROUP), :]
            for pair in range((inner + 1) // 2):
                left = values[:, 2 * pair : 2 * pair + 1]
                right = values[:, 2 * pair + 1 : 2 * pair + 2]
                where = slice(pair * GROUP, (pair + 1) * GROUP)
                scale = 1.0 / (inner + 1)
                leaf_mid[tg, where, :] = jnp.broadcast_to((left + right) * scale, (GROUP, 128))
                leaf_half[tg, where, :] = jnp.broadcast_to((right - left) * scale, (GROUP, 128))

    def start_counts():
        degrees = jnp.broadcast_to(degree[...].astype(F32), (128, rows)).T
        degree_col[...] = degrees
        named_all = jnp.concatenate(
            [neighbour_slot[...], jnp.zeros((128 - entries, rows), jnp.int32)], axis=0
        ).T ^ (m * CAP)
        for j in range(entries):
            named = jnp.broadcast_to(named_all[:, j : j + 1], (rows, 128))
            slot_ids[j] = jnp.where(degrees > j + 0.5, named, -1).astype(jnp.int16)

    def build_counts(first, last):
        one, none = jnp.ones((128, 128), BF16), jnp.zeros((128, 128), BF16)

        @pl.loop(first, last)
        def _(source):
            for half in range(width // 128):
                here = jnp.broadcast_to(lanes + (source * width + half * 128), (128, 128)).astype(
                    jnp.int16
                )
                for part in range(0, rows, 128):
                    total = none
                    for j in range(entries):
                        total = total + jnp.where(slot_ids[j, part : part + 128] == here, one, none)
                    counts[source, part : part + 128, half * 128 : (half + 1) * 128] = total

    def build_rest():
        own_term[...] = (
            jnp.dot(features[...], self_weight[...], preferred_element_type=F32) + hidden_bias[...]
        )
        for place_at, row in enumerate((out_bias, out_gain)):
            wide_row = jnp.concatenate([row[...], jnp.zeros((1, 128 - emb), F32)], axis=1)
            out_cols[place_at] = jnp.broadcast_to(wide_row, (128, 128)).T[:emb]
        for pair in range(leaves // 2):
            emb_t[pair, late_at + emb :, :] = jnp.ones((128 - emb, 2 * rows), BF16)

    def build_margins():
        @pl.loop(0, leaves // 2)
        def _(pair):
            for core in range(2):
                turned = feats[2 * pair + core].T
                where = slice(core * rows, (core + 1) * rows)
                feat_t[:, where] = turned[:EARLY]
                emb_t[pair, 0 : f_in - EARLY, where] = turned[EARLY:]

            for tg in range(groups):
                margins[pair, tg] = jnp.dot(
                    selector[tg, :, :EARLY], feat_t[...], preferred_element_type=F32
                )

    pair_order = (0, 2, 6, 4) if leaves == 8 else tuple(range(0, leaves, 2))
    gather_one(0)
    pl.semaphore_wait(barrier, greeted)

    def send_ids(p):
        pltpu.make_async_remote_copy(
            src_ref=ids.at[0], dst_ref=ids.at[p], send_sem=ids_send, recv_sem=ids_recv.at[p],
            device_id=(g, flip(m, p, leaves)), device_id_type=MESH,
        ).start()

    send_ids(1)
    send_feats(0, 1)
    for axis in range(2):
        send_far_feats(axis)
    send_part(0)

    @pl.loop(2, leaves)
    def _(i):
        send_ids(leaf_order(i))

    for p in pair_order[1:]:
        send_feats(0, p)
    gather_one(1)
    send_part(1)
    build_selector()
    for axis in range(2):
        gather_far(axis)
        send_far(axis)
    start_counts()
    for turn, first in enumerate(pair_order[1:]):
        for p in (first, first + 1):
            gather_one(p)
            send_part(p)
        build_counts(turn * 5, turn * 5 + 5)
    build_counts(15, graphs)
    build_rest()
    build_margins()

    summed[...] = jnp.dot(counts[g], outgoing[g], preferred_element_type=F32)

    def add(source):
        pltpu.make_async_copy(arrived.at[source], arrived.at[source], row_recv.at[source]).wait()
        summed[...] += jnp.dot(counts[source], arrived[source], preferred_element_type=F32)

    @pl.loop(0, 2 * SIDE - 1)
    def _(i):
        low = i // SIDE
        add(spot(2 + low * (near(i % SIDE) - 2), i % SIDE + low * (2 - i % SIDE)))

    @pl.loop(1, 9)
    def _(i):
        add(spot(near(i // 3), near(i % 3)))

    by = jnp.concatenate([degree_col[...]] * (f_in // 128), axis=1)
    mean = (summed[...] / by).astype(BF16)
    hidden = jnp.maximum(
        own_term[...] + jnp.dot(mean, neigh_weight[...], preferred_element_type=F32), 0.0
    ).astype(BF16)
    across = rows // 128
    raw = lax.dot_general(
        out_weight_t[...], hidden, (((1,), (1,)), ((), ())), preferred_element_type=F32
    ) + jnp.concatenate([out_cols[0]] * across, axis=1)
    level = lax.rsqrt(jnp.sum(raw * raw, axis=0, keepdims=True) * (1.0 / emb) + NORM_EPS)
    made_t = raw * level * jnp.concatenate([out_cols[1]] * across, axis=1)
    embedded_t = made_t.astype(BF16)
    emb_t[0, late_at : late_at + emb, 0:rows] = embedded_t

    def emb_slot(p):
        return emb_t.at[p // 2, pl.ds(late_at, emb), pl.ds(pl.multiple_of(p % 2 * rows, rows), rows)]

    @pl.loop(1, leaves)
    def _(i):
        p = leaf_order(i)
        pltpu.make_async_remote_copy(
            src_ref=emb_slot(0), dst_ref=emb_slot(p), send_sem=emb_send.at[p],
            recv_sem=emb_recv.at[p], device_id=(g, flip(m, p, leaves)), device_id_type=MESH,
        ).start()

    embedding_t[...] = embedded_t

    def one_group(pair, tg):
        late = jnp.dot(selector[tg, :, EARLY:], emb_t[pair], preferred_element_type=F32)

        def value(node, part):
            at = place[node] * GROUP
            if 2 * node + 1 >= inner:
                leaf = node - inner // 2
                low = leaf_mid[tg, leaf * GROUP : (leaf + 1) * GROUP, :]
                gap = leaf_half[tg, leaf * GROUP : (leaf + 1) * GROUP, :]
            else:
                left = value(2 * node + 1, part)
                right = value(2 * node + 2, part)
                low = left + right
                gap = right - left
            where = slice(part * 128, (part + 1) * 128)
            turn = jnp.tanh(
                margins[pair, tg, at : at + GROUP, where] + late[at : at + GROUP, where]
            )
            return low + turn * gap

        for core in range(2):
            for part in range(rows // 128):
                total = value(0, core * (rows // 128) + part)
                where = slice(part * 128, (part + 1) * 128)
                partial[2 * pair + core, :, where] += total[:8] + total[8:]

    def arrive(p):
        pltpu.make_async_copy(emb_slot(p), emb_slot(p), emb_recv.at[p]).wait()

    def leave(p):
        pltpu.make_async_remote_copy(
            src_ref=partial.at[p], dst_ref=partial_in.at[p], send_sem=score_send,
            recv_sem=score_recv.at[p], device_id=(g, flip(m, p, leaves)), device_id_type=MESH,
        ).start()

    partial[...] = jnp.zeros(partial.shape, F32)

    @pl.loop(0, leaves // 2)
    def _(i):
        pair = leaf_order(2 * i) // 2

        @pl.when(i > 0)
        def _():
            arrive(2 * pair)

        arrive(2 * pair + 1)
        for tg in range(groups):
            one_group(pair, tg)

        @pl.when(i > 0)
        def _():
            leave(2 * pair)

        leave(2 * pair + 1)

    running = partial[0]
    for p in range(1, leaves):
        pltpu.make_async_copy(partial_in.at[p], partial_in.at[p], score_recv.at[p]).wait()
        running = running + partial_in[p]
    scores[...] = jnp.sum(running, axis=0, keepdims=True)

    others = pl.ds(0, leaves + 1)
    pltpu.make_async_copy(ids.at[others], ids.at[others], ids_send).wait()
    pltpu.make_async_copy(feats.at[others], feats.at[others], feat_send).wait()
    for axis in range(2):
        block = far.at[axis, pl.ds(0, (SIDE - axis) * leaves - 1)]
        pltpu.make_async_copy(block, block, far_send.at[axis]).wait()
    block = outgoing.at[pl.ds(0, 8)]
    pltpu.make_async_copy(block, block, row_send).wait()
    for p in range(1, leaves):
        pltpu.make_async_copy(emb_slot(p), emb_slot(p), emb_send.at[p]).wait()
    block = partial.at[pl.ds(0, leaves - 1)]
    pltpu.make_async_copy(block, block, score_send).wait()


def on_device(
    graphs,
    leaves,
    features,
    send_rows,
    neighbour_slot,
    degree,
    self_weight,
    neigh_weight,
    hidden_bias,
    out_weight,
    out_bias,
    out_gain,
    split_feature,
    threshold,
    leaf_value,
):
    rows, f_in = features.shape
    hid = self_weight.shape[1]
    emb = out_weight.shape[1]
    trees, inner = split_feature.shape
    groups = trees // GROUP
    width = leaves * CAP
    entries = neighbour_slot.shape[1]
    dma = pltpu.SemaphoreType.DMA
    vmem = pl.BlockSpec(memory_space=pltpu.VMEM)
    embedding_t, scores = pl.pallas_call(
        functools.partial(kernel, graphs, leaves),
        out_shape=(
            pltpu.VMEM((emb, rows), BF16),
            pltpu.VMEM((1, rows), F32),
        ),
        in_specs=[vmem] * 13,
        out_specs=(vmem, vmem),
        scratch_shapes=[
            pltpu.VMEM((leaves + 2, rows, f_in), BF16),
            pltpu.VMEM((leaves + 2, CAP, graphs * leaves), jnp.int32),
            pltpu.VMEM((graphs, width, f_in), BF16),
            pltpu.VMEM((2, SIDE * leaves, CAP, f_in), BF16),
            pltpu.VMEM((graphs, width, f_in), BF16),
            pltpu.VMEM((entries, rows, 128), jnp.int16),
            pltpu.VMEM((graphs, rows, width), BF16),
            pltpu.VMEM((groups, inner * GROUP, 512), BF16),
            pltpu.VMEM((groups, (inner + 1) // 2 * GROUP, 128), F32),
            pltpu.VMEM((groups, (inner + 1) // 2 * GROUP, 128), F32),
            pltpu.VMEM((EARLY, 2 * rows), BF16),
            pltpu.VMEM((leaves // 2, 512 - EARLY, 2 * rows), BF16),
            pltpu.VMEM((leaves // 2, groups, inner * GROUP, 2 * rows), F32),
            pltpu.VMEM((rows, hid), F32),
            pltpu.VMEM((2, emb, 128), F32),
            pltpu.VMEM((rows, 128), F32),
            pltpu.VMEM((rows, f_in), F32),
            pltpu.VMEM((leaves, 8, rows), F32),
            pltpu.VMEM((leaves, 8, rows), F32),
            dma,
            dma,
            dma,
            dma((2,)),
            dma((leaves,)),
            dma,
            dma((leaves + 2,)),
            dma((leaves + 2,)),
            dma((graphs,)),
            dma((leaves,)),
            dma((leaves,)),
        ],
        compiler_params=pltpu.CompilerParams(
            collective_id=0, has_side_effects=True, vmem_limit_bytes=62 * 2**20
        ),
        name="sage_forest",
    )(
        features,
        send_rows.reshape(send_rows.shape[1:]).T,
        neighbour_slot.T,
        degree.reshape(1, rows),
        self_weight,
        neigh_weight,
        hidden_bias.reshape(1, hid),
        out_weight.T,
        out_bias.reshape(1, emb),
        out_gain.reshape(1, emb),
        split_feature,
        threshold,
        leaf_value,
    )
    return (embedding_t.T, scores.reshape(rows))


def solution(mesh):
    in_specs = (
        P(("graph", "leaf"), None),
        P(("graph", "leaf"), None, None),
        P(("graph", "leaf"), None),
        P(("graph", "leaf")),
        P(),
        P(),
        P(),
        P(),
        P(),
        P(),
        P("leaf", None),
        P("leaf", None),
        P("leaf", None),
    )
    out_specs = (P(("graph", "leaf"), None), P(("graph", "leaf")))
    return jax.shard_map(
        functools.partial(on_device, mesh.shape["graph"], mesh.shape["leaf"]),
        mesh=mesh,
        in_specs=in_specs,
        out_specs=out_specs,
        check_vma=False,
    )
```

```python
import functools

import jax
import jax.numpy as jnp
from jax import lax
from jax.experimental import pallas as pl
from jax.experimental.pallas import tpu as pltpu
from jax.sharding import PartitionSpec as P

NORM_EPS = 1e-05
CAP = 32
GROUP = 16
SIDE = 4
EARLY = 256
BF16 = jnp.bfloat16
F32 = jnp.float32
MESH = pl.DeviceIdType.MESH


def post_order(inner):
    order = []

    def visit(node):
        if node < inner:
            visit(2 * node + 1)
            visit(2 * node + 2)
            order.append(node)

    visit(0)
    place = [0] * inner
    for position, node in enumerate(order):
        place[node] = position
    return place


def flip(a, b, size):
    total = 0
    bit = 1
    while bit < size:
        total = total + ((a // bit + b // bit) % 2) * bit
        bit *= 2
    return total


def kernel(
    graphs,
    leaves,
    features,
    send_rows,
    neighbour_slot,
    degree,
    self_weight,
    neigh_weight,
    hidden_bias,
    out_weight_t,
    out_bias,
    out_gain,
    split_feature,
    threshold,
    leaf_value,
    embedding_t,
    scores,
    feats,
    ids,
    outgoing,
    far,
    arrived,
    slot_ids,
    counts,
    selector,
    leaf_mid,
    leaf_half,
    feat_t,
    emb_t,
    margins,
    own_term,
    out_cols,
    degree_col,
    summed,
    partial,
    partial_in,
    feat_send,
    ids_send,
    row_send,
    far_send,
    emb_send,
    score_send,
    feat_recv,
    ids_recv,
    row_recv,
    emb_recv,
    score_recv,
):
    g = lax.axis_index("graph")
    m = lax.axis_index("leaf")
    rows, f_in = features.shape
    trees, inner = split_feature.shape
    emb = out_weight_t.shape[0]
    entries = neighbour_slot.shape[0]
    width = leaves * CAP
    groups = trees // GROUP
    place = post_order(inner)
    late_at = f_in - EARLY
    lanes = lax.broadcasted_iota(jnp.int32, (1, 128), 1)

    barrier = pltpu.get_barrier_semaphore()

    x, z = g // SIDE, g % SIDE

    def spot(dx, dz):
        return (x + dx) % SIDE * SIDE + (z + dz) % SIDE

    def near(i):
        return i + i // 2

    def greet(graph, leaf):
        pl.semaphore_signal(barrier, inc=1, device_id=(graph, leaf), device_id_type=MESH)

    @pl.loop(1, SIDE * leaves)
    def _(i):
        greet(spot(0, i // leaves), flip(m, i % leaves, leaves))

    @pl.loop(0, 2 * leaves)
    def _(i):
        greet(spot(1 + 2 * (i // leaves), 0), flip(m, i % leaves, leaves))

    for dx, dz in ((2, 0), (1, 1), (1, 3), (3, 1), (3, 3)):
        greet(spot(dx, dz), m)
    greeted = SIDE * leaves - 1 + 2 * leaves + 5

    devices = graphs * leaves
    ids[0] = send_rows[...]
    feats[0] = features[...]

    def leaf_order(i):
        if leaves == 8:
            return i + 2 * ((i // 4) * (1 - 2 * ((i // 2) % 2)))
        return i

    def send_feats(source, p):
        pltpu.make_async_remote_copy(
            src_ref=feats.at[source],
            dst_ref=feats.at[flip(source, p, leaves)],
            send_sem=feat_send,
            recv_sem=feat_recv.at[flip(source, p, leaves)],
            device_id=(g, flip(m, p, leaves)),
            device_id_type=MESH,
        ).start()

    row_lanes = lax.broadcasted_iota(jnp.int32, (1, rows), 1)

    def gather_one(p):
        if p > 0:
            pltpu.make_async_copy(ids.at[p], ids.at[p], ids_recv.at[p]).wait()
            pltpu.make_async_copy(feats.at[p], feats.at[p], feat_recv.at[p]).wait()
            if p % 2 == 0:
                send_feats(p, 1)
        mine = pltpu.roll(ids[p], devices - m, axis=1)
        picked = pick(mine, range(0, devices, leaves), p)
        for target in range(graphs):
            outgoing[target, pl.ds(p * CAP, CAP), :] = picked[target * CAP : (target + 1) * CAP]

    def pick(mine, columns, slot):
        pieces = []
        for column in columns:
            pieces.append((mine[:, column : column + 1] == row_lanes).astype(F32).astype(BF16))
        return jnp.dot(
            jnp.concatenate(pieces, axis=0), feats[slot], preferred_element_type=F32
        ).astype(BF16)

    def send_part(p):
        @pl.loop(1, 9)
        def _(i):
            target = spot(near(i // 3), near(i % 3))
            part = pl.ds(p * CAP, CAP)
            pltpu.make_async_remote_copy(
                src_ref=outgoing.at[target, part],
                dst_ref=arrived.at[g, part],
                send_sem=row_send,
                recv_sem=row_recv.at[g],
                device_id=(target, m),
                device_id_type=MESH,
            ).start()

    opposite = (spot(2, 0), spot(0, 2))

    def send_far_feats(axis):
        slot = leaves + axis
        for ref, send_sem, recv_sem in ((ids, ids_send, ids_recv), (feats, feat_send, feat_recv)):
            pltpu.make_async_remote_copy(
                src_ref=ref.at[0], dst_ref=ref.at[slot], send_sem=send_sem,
                recv_sem=recv_sem.at[slot], device_id=(opposite[axis], m), device_id_type=MESH,
            ).start()

    def gather_far(axis):
        slot = leaves + axis
        pltpu.make_async_copy(ids.at[slot], ids.at[slot], ids_recv.at[slot]).wait()
        pltpu.make_async_copy(feats.at[slot], feats.at[slot], feat_recv.at[slot]).wait()
        if axis == 0:
            mine = pltpu.roll(ids[slot], devices - x * (SIDE * leaves), axis=1)
            stride = leaves
        else:
            mine = pltpu.roll(ids[slot], devices - z * leaves, axis=1)
            stride = SIDE * leaves
        for half in range(2):
            columns = []
            for other in range(2 * half, 2 * half + 2):
                columns.extend(range(other * stride, other * stride + leaves))
            picked = pick(mine, columns, slot)
            for i in range(2 * leaves):
                far[axis, 2 * leaves * half + i] = picked[i * CAP : (i + 1) * CAP]

    def send_far(axis):
        source = opposite[axis]

        def piece(i):
            turn, p = i // leaves, i % leaves
            if axis == 0:
                graph, other = spot(0, turn), (z + turn) % SIDE
            else:
                graph, other = spot(near(turn), 0), (x + near(turn)) % SIDE
            leaf = flip(m, p, leaves)
            part = pl.ds(p * CAP, CAP)
            return far.at[axis, other * leaves + leaf], arrived.at[source, part], graph, leaf

        here, there, _, _ = piece(0)
        pltpu.make_async_copy(here, there, row_recv.at[source]).start()

        @pl.loop(1, (SIDE - axis) * leaves)
        def _(i):
            src, dst, graph, leaf = piece(i)
            pltpu.make_async_remote_copy(
                src_ref=src, dst_ref=dst, send_sem=far_send.at[axis],
                recv_sem=row_recv.at[source], device_id=(graph, leaf), device_id_type=MESH,
            ).start()

    def build_selector():
        @pl.loop(0, groups)
        def _(tg):
            base = pl.multiple_of(tg * GROUP, GROUP)
            node_ids = split_feature[pl.ds(base, GROUP), :]
            cuts = threshold[pl.ds(base, GROUP), :]
            high = cuts.astype(BF16).astype(F32)
            middle = (cuts - high).astype(BF16).astype(F32)
            low = cuts - high - middle
            for node in range(inner):
                column = jnp.broadcast_to(node_ids[:, node : node + 1], (GROUP, 128))
                parts = []
                for q in range(4):
                    parts.append(jnp.where(column == lanes + q * 128, 1.0, 0.0))
                last = parts[3]
                for extra, part in enumerate((high, middle, low)):
                    last = jnp.where(lanes == 64 + extra, -part[:, node : node + 1], last)
                parts[3] = last
                selector[tg, place[node] * GROUP : (place[node] + 1) * GROUP, :] = jnp.concatenate(
                    parts, axis=1
                ).astype(BF16)
            values = leaf_value[pl.ds(base, GROUP), :]
            for pair in range((inner + 1) // 2):
                left = values[:, 2 * pair : 2 * pair + 1]
                right = values[:, 2 * pair + 1 : 2 * pair + 2]
                where = slice(pair * GROUP, (pair + 1) * GROUP)
                scale = 1.0 / (inner + 1)
                leaf_mid[tg, where, :] = jnp.broadcast_to((left + right) * scale, (GROUP, 128))
                leaf_half[tg, where, :] = jnp.broadcast_to((right - left) * scale, (GROUP, 128))

    def start_counts():
        degrees = jnp.broadcast_to(degree[...].astype(F32), (128, rows)).T
        degree_col[...] = degrees
        named_all = jnp.concatenate(
            [neighbour_slot[...], jnp.zeros((128 - entries, rows), jnp.int32)], axis=0
        ).T ^ (m * CAP)
        for j in range(entries):
            named = jnp.broadcast_to(named_all[:, j : j + 1], (rows, 128))
            slot_ids[j] = jnp.where(degrees > j + 0.5, named, -1).astype(jnp.int16)

    def build_counts(first, last):
        one, none = jnp.ones((128, 128), BF16), jnp.zeros((128, 128), BF16)

        @pl.loop(first, last)
        def _(source):
            for half in range(width // 128):
                here = jnp.broadcast_to(lanes + (source * width + half * 128), (128, 128)).astype(
                    jnp.int16
                )
                for part in range(0, rows, 128):
                    total = none
                    for j in range(entries):
                        total = total + jnp.where(slot_ids[j, part : part + 128] == here, one, none)
                    counts[source, part : part + 128, half * 128 : (half + 1) * 128] = total

    def build_rest():
        own_term[...] = (
            jnp.dot(features[...], self_weight[...], preferred_element_type=F32) + hidden_bias[...]
        )
        for place_at, row in enumerate((out_bias, out_gain)):
            wide_row = jnp.concatenate([row[...], jnp.zeros((1, 128 - emb), F32)], axis=1)
            out_cols[place_at] = jnp.broadcast_to(wide_row, (128, 128)).T[:emb]
        for pair in range(leaves // 2):
            emb_t[pair, late_at + emb :, :] = jnp.ones((128 - emb, 2 * rows), BF16)

    def build_margins():
        @pl.loop(0, leaves // 2)
        def _(pair):
            for core in range(2):
                turned = feats[2 * pair + core].T
                where = slice(core * rows, (core + 1) * rows)
                feat_t[:, where] = turned[:EARLY]
                emb_t[pair, 0 : f_in - EARLY, where] = turned[EARLY:]

            for tg in range(groups):
                margins[pair, tg] = jnp.dot(
                    selector[tg, :, :EARLY], feat_t[...], preferred_element_type=F32
                )

    pair_order = (0, 2, 6, 4) if leaves == 8 else tuple(range(0, leaves, 2))
    gather_one(0)
    pl.semaphore_wait(barrier, greeted)

    def send_ids(p):
        pltpu.make_async_remote_copy(
            src_ref=ids.at[0], dst_ref=ids.at[p], send_sem=ids_send, recv_sem=ids_recv.at[p],
            device_id=(g, flip(m, p, leaves)), device_id_type=MESH,
        ).start()

    send_ids(1)
    send_feats(0, 1)
    for axis in range(2):
        send_far_feats(axis)
    send_part(0)

    @pl.loop(2, leaves)
    def _(i):
        send_ids(leaf_order(i))

    for p in pair_order[1:]:
        send_feats(0, p)
    gather_one(1)
    send_part(1)
    build_selector()
    for axis in range(2):
        gather_far(axis)
        send_far(axis)
    start_counts()
    for turn, first in enumerate(pair_order[1:]):
        for p in (first, first + 1):
            gather_one(p)
            send_part(p)
        build_counts(turn * 5, turn * 5 + 5)
    build_counts(15, graphs)
    build_rest()
    build_margins()

    summed[...] = jnp.dot(counts[g], outgoing[g], preferred_element_type=F32)

    def add_all(total, sources):
        for source in sources:
            pltpu.make_async_copy(
                arrived.at[source], arrived.at[source], row_recv.at[source]
            ).wait()
        for source in sources:
            total = total + jnp.dot(
                counts[source], arrived[source], preferred_element_type=F32
            )
        return total

    steps = (0, 1, 3)
    summed[...] = add_all(
        summed[...], [spot(2, dz) for dz in range(SIDE)] + [spot(dx, 2) for dx in steps]
    )
    hops = [spot(dx, dz) for dx in steps for dz in steps][1:]
    summed[...] = add_all(summed[...], hops)

    by = jnp.concatenate([degree_col[...]] * (f_in // 128), axis=1)
    mean = (summed[...] / by).astype(BF16)
    hidden = jnp.maximum(
        own_term[...] + jnp.dot(mean, neigh_weight[...], preferred_element_type=F32), 0.0
    ).astype(BF16)
    across = rows // 128
    raw = lax.dot_general(
        out_weight_t[...], hidden, (((1,), (1,)), ((), ())), preferred_element_type=F32
    ) + jnp.concatenate([out_cols[0]] * across, axis=1)
    level = lax.rsqrt(jnp.sum(raw * raw, axis=0, keepdims=True) * (1.0 / emb) + NORM_EPS)
    made_t = raw * level * jnp.concatenate([out_cols[1]] * across, axis=1)
    embedded_t = made_t.astype(BF16)
    emb_t[0, late_at : late_at + emb, 0:rows] = embedded_t

    def emb_slot(p):
        return emb_t.at[p // 2, pl.ds(late_at, emb), pl.ds(pl.multiple_of(p % 2 * rows, rows), rows)]

    @pl.loop(1, leaves)
    def _(i):
        p = leaf_order(i)
        pltpu.make_async_remote_copy(
            src_ref=emb_slot(0), dst_ref=emb_slot(p), send_sem=emb_send.at[p],
            recv_sem=emb_recv.at[p], device_id=(g, flip(m, p, leaves)), device_id_type=MESH,
        ).start()

    embedding_t[...] = embedded_t

    def one_group(pair, tg):
        late = jnp.dot(selector[tg, :, EARLY:], emb_t[pair], preferred_element_type=F32)

        def value(node, part):
            at = place[node] * GROUP
            if 2 * node + 1 >= inner:
                leaf = node - inner // 2
                low = leaf_mid[tg, leaf * GROUP : (leaf + 1) * GROUP, :]
                gap = leaf_half[tg, leaf * GROUP : (leaf + 1) * GROUP, :]
            else:
                left = value(2 * node + 1, part)
                right = value(2 * node + 2, part)
                low = left + right
                gap = right - left
            where = slice(part * 128, (part + 1) * 128)
            turn = jnp.tanh(
                margins[pair, tg, at : at + GROUP, where] + late[at : at + GROUP, where]
            )
            return low + turn * gap

        for core in range(2):
            for part in range(rows // 128):
                total = value(0, core * (rows // 128) + part)
                where = slice(part * 128, (part + 1) * 128)
                partial[2 * pair + core, :, where] += total[:8] + total[8:]

    def arrive(p):
        pltpu.make_async_copy(emb_slot(p), emb_slot(p), emb_recv.at[p]).wait()

    def leave(p):
        pltpu.make_async_remote_copy(
            src_ref=partial.at[p], dst_ref=partial_in.at[p], send_sem=score_send,
            recv_sem=score_recv.at[p], device_id=(g, flip(m, p, leaves)), device_id_type=MESH,
        ).start()

    partial[...] = jnp.zeros(partial.shape, F32)

    @pl.loop(0, leaves // 2)
    def _(i):
        pair = leaf_order(2 * i) // 2

        @pl.when(i > 0)
        def _():
            arrive(2 * pair)

        arrive(2 * pair + 1)
        for tg in range(groups):
            one_group(pair, tg)

        @pl.when(i > 0)
        def _():
            leave(2 * pair)

        leave(2 * pair + 1)

    running = partial[0]
    for p in range(1, leaves):
        pltpu.make_async_copy(partial_in.at[p], partial_in.at[p], score_recv.at[p]).wait()
        running = running + partial_in[p]
    scores[...] = jnp.sum(running, axis=0, keepdims=True)

    others = pl.ds(0, leaves + 1)
    pltpu.make_async_copy(ids.at[others], ids.at[others], ids_send).wait()
    pltpu.make_async_copy(feats.at[others], feats.at[others], feat_send).wait()
    for axis in range(2):
        block = far.at[axis, pl.ds(0, (SIDE - axis) * leaves - 1)]
        pltpu.make_async_copy(block, block, far_send.at[axis]).wait()
    block = outgoing.at[pl.ds(0, 8)]
    pltpu.make_async_copy(block, block, row_send).wait()
    for p in range(1, leaves):
        pltpu.make_async_copy(emb_slot(p), emb_slot(p), emb_send.at[p]).wait()
    block = partial.at[pl.ds(0, leaves - 1)]
    pltpu.make_async_copy(block, block, score_send).wait()


def on_device(
    graphs,
    leaves,
    features,
    send_rows,
    neighbour_slot,
    degree,
    self_weight,
    neigh_weight,
    hidden_bias,
    out_weight,
    out_bias,
    out_gain,
    split_feature,
    threshold,
    leaf_value,
):
    rows, f_in = features.shape
    hid = self_weight.shape[1]
    emb = out_weight.shape[1]
    trees, inner = split_feature.shape
    groups = trees // GROUP
    width = leaves * CAP
    entries = neighbour_slot.shape[1]
    dma = pltpu.SemaphoreType.DMA
    vmem = pl.BlockSpec(memory_space=pltpu.VMEM)
    embedding_t, scores = pl.pallas_call(
        functools.partial(kernel, graphs, leaves),
        out_shape=(
            pltpu.VMEM((emb, rows), BF16),
            pltpu.VMEM((1, rows), F32),
        ),
        in_specs=[vmem] * 13,
        out_specs=(vmem, vmem),
        scratch_shapes=[
            pltpu.VMEM((leaves + 2, rows, f_in), BF16),
            pltpu.VMEM((leaves + 2, CAP, graphs * leaves), jnp.int32),
            pltpu.VMEM((graphs, width, f_in), BF16),
            pltpu.VMEM((2, SIDE * leaves, CAP, f_in), BF16),
            pltpu.VMEM((graphs, width, f_in), BF16),
            pltpu.VMEM((entries, rows, 128), jnp.int16),
            pltpu.VMEM((graphs, rows, width), BF16),
            pltpu.VMEM((groups, inner * GROUP, 512), BF16),
            pltpu.VMEM((groups, (inner + 1) // 2 * GROUP, 128), F32),
            pltpu.VMEM((groups, (inner + 1) // 2 * GROUP, 128), F32),
            pltpu.VMEM((EARLY, 2 * rows), BF16),
            pltpu.VMEM((leaves // 2, 512 - EARLY, 2 * rows), BF16),
            pltpu.VMEM((leaves // 2, groups, inner * GROUP, 2 * rows), F32),
            pltpu.VMEM((rows, hid), F32),
            pltpu.VMEM((2, emb, 128), F32),
            pltpu.VMEM((rows, 128), F32),
            pltpu.VMEM((rows, f_in), F32),
            pltpu.VMEM((leaves, 8, rows), F32),
            pltpu.VMEM((leaves, 8, rows), F32),
            dma,
            dma,
            dma,
            dma((2,)),
            dma((leaves,)),
            dma,
            dma((leaves + 2,)),
            dma((leaves + 2,)),
            dma((graphs,)),
            dma((leaves,)),
            dma((leaves,)),
        ],
        compiler_params=pltpu.CompilerParams(
            collective_id=0, has_side_effects=True, vmem_limit_bytes=62 * 2**20
        ),
        name="sage_forest",
    )(
        features,
        send_rows.reshape(send_rows.shape[1:]).T,
        neighbour_slot.T,
        degree.reshape(1, rows),
        self_weight,
        neigh_weight,
        hidden_bias.reshape(1, hid),
        out_weight.T,
        out_bias.reshape(1, emb),
        out_gain.reshape(1, emb),
        split_feature,
        threshold,
        leaf_value,
    )
    return (embedding_t.T, scores.reshape(rows))


def solution(mesh):
    in_specs = (
        P(("graph", "leaf"), None),
        P(("graph", "leaf"), None, None),
        P(("graph", "leaf"), None),
        P(("graph", "leaf")),
        P(),
        P(),
        P(),
        P(),
        P(),
        P(),
        P("leaf", None),
        P("leaf", None),
        P("leaf", None),
    )
    out_specs = (P(("graph", "leaf"), None), P(("graph", "leaf")))
    return jax.shard_map(
        functools.partial(on_device, mesh.shape["graph"], mesh.shape["leaf"]),
        mesh=mesh,
        in_specs=in_specs,
        out_specs=out_specs,
        check_vma=False,
    )
```

```python
import functools

import jax
import jax.numpy as jnp
from jax import lax
from jax.experimental import pallas as pl
from jax.experimental.pallas import tpu as pltpu
from jax.sharding import PartitionSpec as P

NORM_EPS = 1e-05
CAP = 32
GROUP = 16
SIDE = 4
EARLY = 256
BF16 = jnp.bfloat16
F32 = jnp.float32
MESH = pl.DeviceIdType.MESH


def post_order(inner):
    order = []

    def visit(node):
        if node < inner:
            visit(2 * node + 1)
            visit(2 * node + 2)
            order.append(node)

    visit(0)
    place = [0] * inner
    for position, node in enumerate(order):
        place[node] = position
    return place


def flip(a, b, size):
    total = 0
    bit = 1
    while bit < size:
        total = total + ((a // bit + b // bit) % 2) * bit
        bit *= 2
    return total


def kernel(
    graphs,
    leaves,
    features,
    send_rows,
    neighbour_slot,
    degree,
    self_weight,
    neigh_weight,
    hidden_bias,
    out_weight_t,
    out_bias,
    out_gain,
    split_feature,
    threshold,
    leaf_value,
    embedding_t,
    scores,
    feats,
    ids,
    outgoing,
    far,
    arrived,
    slot_ids,
    counts,
    selector,
    leaf_mid,
    leaf_half,
    feat_t,
    emb_t,
    margins,
    own_term,
    out_cols,
    degree_col,
    summed,
    partial,
    partial_in,
    feat_send,
    ids_send,
    row_send,
    far_send,
    emb_send,
    score_send,
    feat_recv,
    ids_recv,
    row_recv,
    emb_recv,
    score_recv,
):
    g = lax.axis_index("graph")
    m = lax.axis_index("leaf")
    rows, f_in = features.shape
    trees, inner = split_feature.shape
    emb = out_weight_t.shape[0]
    entries = neighbour_slot.shape[0]
    width = leaves * CAP
    groups = trees // GROUP
    place = post_order(inner)
    late_at = f_in - EARLY
    lanes = lax.broadcasted_iota(jnp.int32, (1, 128), 1)

    barrier = pltpu.get_barrier_semaphore()

    x, z = g // SIDE, g % SIDE

    def spot(dx, dz):
        return (x + dx) % SIDE * SIDE + (z + dz) % SIDE

    def near(i):
        return i + i // 2

    def greet(graph, leaf):
        pl.semaphore_signal(barrier, inc=1, device_id=(graph, leaf), device_id_type=MESH)

    for i in range(1, SIDE * leaves):
        greet(spot(0, i // leaves), flip(m, i % leaves, leaves))

    for i in range(2 * leaves):
        greet(spot(1 + 2 * (i // leaves), 0), flip(m, i % leaves, leaves))

    for dx, dz in ((2, 0), (1, 1), (1, 3), (3, 1), (3, 3)):
        greet(spot(dx, dz), m)
    greeted = SIDE * leaves - 1 + 2 * leaves + 5

    devices = graphs * leaves
    ids[0] = send_rows[...]
    feats[0] = features[...]

    def leaf_order(i):
        if leaves == 8:
            return i + 2 * ((i // 4) * (1 - 2 * ((i // 2) % 2)))
        return i

    def send_feats(source, p):
        pltpu.make_async_remote_copy(
            src_ref=feats.at[source],
            dst_ref=feats.at[flip(source, p, leaves)],
            send_sem=feat_send,
            recv_sem=feat_recv.at[flip(source, p, leaves)],
            device_id=(g, flip(m, p, leaves)),
            device_id_type=MESH,
        ).start()

    row_lanes = lax.broadcasted_iota(jnp.int32, (1, rows), 1)

    def gather_one(p):
        if p > 0:
            pltpu.make_async_copy(ids.at[p], ids.at[p], ids_recv.at[p]).wait()
            pltpu.make_async_copy(feats.at[p], feats.at[p], feat_recv.at[p]).wait()
            if p % 2 == 0:
                send_feats(p, 1)
        mine = pltpu.roll(ids[p], devices - m, axis=1)
        picked = pick(mine, range(0, devices, leaves), p)
        for target in range(graphs):
            outgoing[target, pl.ds(p * CAP, CAP), :] = picked[target * CAP : (target + 1) * CAP]

    def pick(mine, columns, slot):
        pieces = []
        for column in columns:
            pieces.append((mine[:, column : column + 1] == row_lanes).astype(F32).astype(BF16))
        return jnp.dot(
            jnp.concatenate(pieces, axis=0), feats[slot], preferred_element_type=F32
        ).astype(BF16)

    def send_part(p):
        for i in range(1, 9):
            target = spot(near(i // 3), near(i % 3))
            part = pl.ds(p * CAP, CAP)
            pltpu.make_async_remote_copy(
                src_ref=outgoing.at[target, part],
                dst_ref=arrived.at[g, part],
                send_sem=row_send,
                recv_sem=row_recv.at[g],
                device_id=(target, m),
                device_id_type=MESH,
            ).start()

    opposite = (spot(2, 0), spot(0, 2))

    def send_far_feats(axis):
        slot = leaves + axis
        for ref, send_sem, recv_sem in ((ids, ids_send, ids_recv), (feats, feat_send, feat_recv)):
            pltpu.make_async_remote_copy(
                src_ref=ref.at[0], dst_ref=ref.at[slot], send_sem=send_sem,
                recv_sem=recv_sem.at[slot], device_id=(opposite[axis], m), device_id_type=MESH,
            ).start()

    def gather_far(axis):
        slot = leaves + axis
        pltpu.make_async_copy(ids.at[slot], ids.at[slot], ids_recv.at[slot]).wait()
        pltpu.make_async_copy(feats.at[slot], feats.at[slot], feat_recv.at[slot]).wait()
        if axis == 0:
            mine = pltpu.roll(ids[slot], devices - x * (SIDE * leaves), axis=1)
            stride = leaves
        else:
            mine = pltpu.roll(ids[slot], devices - z * leaves, axis=1)
            stride = SIDE * leaves
        for half in range(2):
            columns = []
            for other in range(2 * half, 2 * half + 2):
                columns.extend(range(other * stride, other * stride + leaves))
            picked = pick(mine, columns, slot)
            for i in range(2 * leaves):
                far[axis, 2 * leaves * half + i] = picked[i * CAP : (i + 1) * CAP]

    def send_far(axis):
        source = opposite[axis]

        def piece(i):
            turn, p = i // leaves, i % leaves
            if axis == 0:
                graph, other = spot(0, turn), (z + turn) % SIDE
            else:
                graph, other = spot(near(turn), 0), (x + near(turn)) % SIDE
            leaf = flip(m, p, leaves)
            part = pl.ds(p * CAP, CAP)
            return far.at[axis, other * leaves + leaf], arrived.at[source, part], graph, leaf

        here, there, _, _ = piece(0)
        pltpu.make_async_copy(here, there, row_recv.at[source]).start()

        for i in range(1, (SIDE - axis) * leaves):
            src, dst, graph, leaf = piece(i)
            pltpu.make_async_remote_copy(
                src_ref=src, dst_ref=dst, send_sem=far_send.at[axis],
                recv_sem=row_recv.at[source], device_id=(graph, leaf), device_id_type=MESH,
            ).start()

    def build_selector():
        @pl.loop(0, groups)
        def _(tg):
            base = pl.multiple_of(tg * GROUP, GROUP)
            node_ids = split_feature[pl.ds(base, GROUP), :]
            cuts = threshold[pl.ds(base, GROUP), :]
            high = cuts.astype(BF16).astype(F32)
            middle = (cuts - high).astype(BF16).astype(F32)
            low = cuts - high - middle
            for node in range(inner):
                column = jnp.broadcast_to(node_ids[:, node : node + 1], (GROUP, 128))
                parts = []
                for q in range(4):
                    parts.append(jnp.where(column == lanes + q * 128, 1.0, 0.0))
                last = parts[3]
                for extra, part in enumerate((high, middle, low)):
                    last = jnp.where(lanes == 64 + extra, -part[:, node : node + 1], last)
                parts[3] = last
                selector[tg, place[node] * GROUP : (place[node] + 1) * GROUP, :] = jnp.concatenate(
                    parts, axis=1
                ).astype(BF16)
            values = leaf_value[pl.ds(base, GROUP), :]
            for pair in range((inner + 1) // 2):
                left = values[:, 2 * pair : 2 * pair + 1]
                right = values[:, 2 * pair + 1 : 2 * pair + 2]
                where = slice(pair * GROUP, (pair + 1) * GROUP)
                scale = 1.0 / (inner + 1)
                leaf_mid[tg, where, :] = jnp.broadcast_to((left + right) * scale, (GROUP, 128))
                leaf_half[tg, where, :] = jnp.broadcast_to((right - left) * scale, (GROUP, 128))

    def start_counts():
        degrees = jnp.broadcast_to(degree[...].astype(F32), (128, rows)).T
        degree_col[...] = degrees
        named_all = jnp.concatenate(
            [neighbour_slot[...], jnp.zeros((128 - entries, rows), jnp.int32)], axis=0
        ).T ^ (m * CAP)
        for j in range(entries):
            named = jnp.broadcast_to(named_all[:, j : j + 1], (rows, 128))
            slot_ids[j] = jnp.where(degrees > j + 0.5, named, -1).astype(jnp.int16)

    def build_counts(first, last):
        one, none = jnp.ones((128, 128), BF16), jnp.zeros((128, 128), BF16)

        @pl.loop(first, last)
        def _(source):
            for half in range(width // 128):
                here = jnp.broadcast_to(lanes + (source * width + half * 128), (128, 128)).astype(
                    jnp.int16
                )
                for part in range(0, rows, 128):
                    total = none
                    for j in range(entries):
                        total = total + jnp.where(slot_ids[j, part : part + 128] == here, one, none)
                    counts[source, part : part + 128, half * 128 : (half + 1) * 128] = total

    def build_rest():
        own_term[...] = (
            jnp.dot(features[...], self_weight[...], preferred_element_type=F32) + hidden_bias[...]
        )
        for place_at, row in enumerate((out_bias, out_gain)):
            wide_row = jnp.concatenate([row[...], jnp.zeros((1, 128 - emb), F32)], axis=1)
            out_cols[place_at] = jnp.broadcast_to(wide_row, (128, 128)).T[:emb]
        for pair in range(leaves // 2):
            emb_t[pair, late_at + emb :, :] = jnp.ones((128 - emb, 2 * rows), BF16)

    def build_margins():
        @pl.loop(0, leaves // 2)
        def _(pair):
            for core in range(2):
                turned = feats[2 * pair + core].T
                where = slice(core * rows, (core + 1) * rows)
                feat_t[:, where] = turned[:EARLY]
                emb_t[pair, 0 : f_in - EARLY, where] = turned[EARLY:]

            for tg in range(groups):
                margins[pair, tg] = jnp.dot(
                    selector[tg, :, :EARLY], feat_t[...], preferred_element_type=F32
                )

    pair_order = (0, 2, 6, 4) if leaves == 8 else tuple(range(0, leaves, 2))
    gather_one(0)
    pl.semaphore_wait(barrier, greeted)

    def send_ids(p):
        pltpu.make_async_remote_copy(
            src_ref=ids.at[0], dst_ref=ids.at[p], send_sem=ids_send, recv_sem=ids_recv.at[p],
            device_id=(g, flip(m, p, leaves)), device_id_type=MESH,
        ).start()

    send_ids(1)
    send_feats(0, 1)
    for axis in range(2):
        send_far_feats(axis)
    send_part(0)

    for i in range(2, leaves):
        send_ids(leaf_order(i))

    for p in pair_order[1:]:
        send_feats(0, p)
    gather_one(1)
    send_part(1)
    build_selector()
    for axis in range(2):
        gather_far(axis)
        send_far(axis)
    start_counts()
    for turn, first in enumerate(pair_order[1:]):
        for p in (first, first + 1):
            gather_one(p)
            send_part(p)
        build_counts(turn * 5, turn * 5 + 5)
    build_counts(15, graphs)
    build_rest()
    build_margins()

    summed[...] = jnp.dot(counts[g], outgoing[g], preferred_element_type=F32)

    def add_all(total, sources):
        for source in sources:
            pltpu.make_async_copy(
                arrived.at[source], arrived.at[source], row_recv.at[source]
            ).wait()
        for source in sources:
            total = total + jnp.dot(
                counts[source], arrived[source], preferred_element_type=F32
            )
        return total

    steps = (0, 1, 3)
    summed[...] = add_all(
        summed[...], [spot(2, dz) for dz in range(SIDE)] + [spot(dx, 2) for dx in steps]
    )
    hops = [spot(dx, dz) for dx in steps for dz in steps][1:]
    summed[...] = add_all(summed[...], hops)

    by = jnp.concatenate([degree_col[...]] * (f_in // 128), axis=1)
    mean = (summed[...] / by).astype(BF16)
    hidden = jnp.maximum(
        own_term[...] + jnp.dot(mean, neigh_weight[...], preferred_element_type=F32), 0.0
    ).astype(BF16)
    across = rows // 128
    raw = lax.dot_general(
        out_weight_t[...], hidden, (((1,), (1,)), ((), ())), preferred_element_type=F32
    ) + jnp.concatenate([out_cols[0]] * across, axis=1)
    level = lax.rsqrt(jnp.sum(raw * raw, axis=0, keepdims=True) * (1.0 / emb) + NORM_EPS)
    made_t = raw * level * jnp.concatenate([out_cols[1]] * across, axis=1)
    embedded_t = made_t.astype(BF16)
    emb_t[0, late_at : late_at + emb, 0:rows] = embedded_t

    def emb_slot(p):
        return emb_t.at[p // 2, pl.ds(late_at, emb), pl.ds(p % 2 * rows if isinstance(p, int) else pl.multiple_of(p % 2 * rows, rows), rows)]

    for i in range(1, leaves):
        p = leaf_order(i)
        pltpu.make_async_remote_copy(
            src_ref=emb_slot(0), dst_ref=emb_slot(p), send_sem=emb_send.at[p],
            recv_sem=emb_recv.at[p], device_id=(g, flip(m, p, leaves)), device_id_type=MESH,
        ).start()

    embedding_t[...] = embedded_t

    def one_group(pair, tg):
        late = jnp.dot(selector[tg, :, EARLY:], emb_t[pair], preferred_element_type=F32)

        def value(node, part):
            at = place[node] * GROUP
            if 2 * node + 1 >= inner:
                leaf = node - inner // 2
                low = leaf_mid[tg, leaf * GROUP : (leaf + 1) * GROUP, :]
                gap = leaf_half[tg, leaf * GROUP : (leaf + 1) * GROUP, :]
            else:
                left = value(2 * node + 1, part)
                right = value(2 * node + 2, part)
                low = left + right
                gap = right - left
            where = slice(part * 128, (part + 1) * 128)
            turn = jnp.tanh(
                margins[pair, tg, at : at + GROUP, where] + late[at : at + GROUP, where]
            )
            return low + turn * gap

        for core in range(2):
            for part in range(rows // 128):
                total = value(0, core * (rows // 128) + part)
                where = slice(part * 128, (part + 1) * 128)
                partial[2 * pair + core, :, where] += total[:8] + total[8:]

    def arrive(p):
        pltpu.make_async_copy(emb_slot(p), emb_slot(p), emb_recv.at[p]).wait()

    def leave(p):
        pltpu.make_async_remote_copy(
            src_ref=partial.at[p], dst_ref=partial_in.at[p], send_sem=score_send,
            recv_sem=score_recv.at[p], device_id=(g, flip(m, p, leaves)), device_id_type=MESH,
        ).start()

    partial[...] = jnp.zeros(partial.shape, F32)

    @pl.loop(0, leaves // 2)
    def _(i):
        pair = leaf_order(2 * i) // 2

        @pl.when(i > 0)
        def _():
            arrive(2 * pair)

        arrive(2 * pair + 1)
        for tg in range(groups):
            one_group(pair, tg)

        @pl.when(i > 0)
        def _():
            leave(2 * pair)

        leave(2 * pair + 1)

    running = partial[0]
    for p in range(1, leaves):
        pltpu.make_async_copy(partial_in.at[p], partial_in.at[p], score_recv.at[p]).wait()
        running = running + partial_in[p]
    scores[...] = jnp.sum(running, axis=0, keepdims=True)

    others = pl.ds(0, leaves + 1)
    pltpu.make_async_copy(ids.at[others], ids.at[others], ids_send).wait()
    pltpu.make_async_copy(feats.at[others], feats.at[others], feat_send).wait()
    for axis in range(2):
        block = far.at[axis, pl.ds(0, (SIDE - axis) * leaves - 1)]
        pltpu.make_async_copy(block, block, far_send.at[axis]).wait()
    block = outgoing.at[pl.ds(0, 8)]
    pltpu.make_async_copy(block, block, row_send).wait()
    for p in range(1, leaves):
        pltpu.make_async_copy(emb_slot(p), emb_slot(p), emb_send.at[p]).wait()
    block = partial.at[pl.ds(0, leaves - 1)]
    pltpu.make_async_copy(block, block, score_send).wait()


def on_device(
    graphs,
    leaves,
    features,
    send_rows,
    neighbour_slot,
    degree,
    self_weight,
    neigh_weight,
    hidden_bias,
    out_weight,
    out_bias,
    out_gain,
    split_feature,
    threshold,
    leaf_value,
):
    rows, f_in = features.shape
    hid = self_weight.shape[1]
    emb = out_weight.shape[1]
    trees, inner = split_feature.shape
    groups = trees // GROUP
    width = leaves * CAP
    entries = neighbour_slot.shape[1]
    dma = pltpu.SemaphoreType.DMA
    vmem = pl.BlockSpec(memory_space=pltpu.VMEM)
    embedding_t, scores = pl.pallas_call(
        functools.partial(kernel, graphs, leaves),
        out_shape=(
            pltpu.VMEM((emb, rows), BF16),
            pltpu.VMEM((1, rows), F32),
        ),
        in_specs=[vmem] * 13,
        out_specs=(vmem, vmem),
        scratch_shapes=[
            pltpu.VMEM((leaves + 2, rows, f_in), BF16),
            pltpu.VMEM((leaves + 2, CAP, graphs * leaves), jnp.int32),
            pltpu.VMEM((graphs, width, f_in), BF16),
            pltpu.VMEM((2, SIDE * leaves, CAP, f_in), BF16),
            pltpu.VMEM((graphs, width, f_in), BF16),
            pltpu.VMEM((entries, rows, 128), jnp.int16),
            pltpu.VMEM((graphs, rows, width), BF16),
            pltpu.VMEM((groups, inner * GROUP, 512), BF16),
            pltpu.VMEM((groups, (inner + 1) // 2 * GROUP, 128), F32),
            pltpu.VMEM((groups, (inner + 1) // 2 * GROUP, 128), F32),
            pltpu.VMEM((EARLY, 2 * rows), BF16),
            pltpu.VMEM((leaves // 2, 512 - EARLY, 2 * rows), BF16),
            pltpu.VMEM((leaves // 2, groups, inner * GROUP, 2 * rows), F32),
            pltpu.VMEM((rows, hid), F32),
            pltpu.VMEM((2, emb, 128), F32),
            pltpu.VMEM((rows, 128), F32),
            pltpu.VMEM((rows, f_in), F32),
            pltpu.VMEM((leaves, 8, rows), F32),
            pltpu.VMEM((leaves, 8, rows), F32),
            dma,
            dma,
            dma,
            dma((2,)),
            dma((leaves,)),
            dma,
            dma((leaves + 2,)),
            dma((leaves + 2,)),
            dma((graphs,)),
            dma((leaves,)),
            dma((leaves,)),
        ],
        compiler_params=pltpu.CompilerParams(
            collective_id=0, has_side_effects=True, vmem_limit_bytes=62 * 2**20
        ),
        name="sage_forest",
    )(
        features,
        send_rows.reshape(send_rows.shape[1:]).T,
        neighbour_slot.T,
        degree.reshape(1, rows),
        self_weight,
        neigh_weight,
        hidden_bias.reshape(1, hid),
        out_weight.T,
        out_bias.reshape(1, emb),
        out_gain.reshape(1, emb),
        split_feature,
        threshold,
        leaf_value,
    )
    return (embedding_t.T, scores.reshape(rows))


def solution(mesh):
    in_specs = (
        P(("graph", "leaf"), None),
        P(("graph", "leaf"), None, None),
        P(("graph", "leaf"), None),
        P(("graph", "leaf")),
        P(),
        P(),
        P(),
        P(),
        P(),
        P(),
        P("leaf", None),
        P("leaf", None),
        P("leaf", None),
    )
    out_specs = (P(("graph", "leaf"), None), P(("graph", "leaf")))
    return jax.shard_map(
        functools.partial(on_device, mesh.shape["graph"], mesh.shape["leaf"]),
        mesh=mesh,
        in_specs=in_specs,
        out_specs=out_specs,
        check_vma=False,
    )
```

```python
import functools

import jax
import jax.numpy as jnp
from jax import lax
from jax.experimental import pallas as pl
from jax.experimental.pallas import tpu as pltpu
from jax.sharding import PartitionSpec as P

NORM_EPS = 1e-05
CAP = 32
GROUP = 16
SIDE = 4
EARLY = 256
BF16 = jnp.bfloat16
F32 = jnp.float32
MESH = pl.DeviceIdType.MESH


def post_order(inner):
    order = []

    def visit(node):
        if node < inner:
            visit(2 * node + 1)
            visit(2 * node + 2)
            order.append(node)

    visit(0)
    place = [0] * inner
    for position, node in enumerate(order):
        place[node] = position
    return place


def flip(a, b, size):
    total = 0
    bit = 1
    while bit < size:
        total = total + ((a // bit + b // bit) % 2) * bit
        bit *= 2
    return total


def kernel(
    graphs,
    leaves,
    features,
    send_rows,
    neighbour_slot,
    degree,
    self_weight,
    neigh_weight,
    hidden_bias,
    out_weight_t,
    out_bias,
    out_gain,
    split_feature,
    threshold,
    leaf_value,
    embedding_t,
    scores,
    feats,
    ids,
    outgoing,
    far,
    arrived,
    slot_ids,
    counts,
    selector,
    leaf_mid,
    leaf_half,
    feat_t,
    emb_t,
    margins,
    own_term,
    out_cols,
    degree_col,
    summed,
    partial,
    partial_in,
    feat_send,
    ids_send,
    row_send,
    far_send,
    emb_send,
    score_send,
    feat_recv,
    ids_recv,
    row_recv,
    emb_recv,
    score_recv,
):
    g = lax.axis_index("graph")
    m = lax.axis_index("leaf")
    rows, f_in = features.shape
    trees, inner = split_feature.shape
    emb = out_weight_t.shape[0]
    entries = neighbour_slot.shape[0]
    width = leaves * CAP
    groups = trees // GROUP
    place = post_order(inner)
    late_at = f_in - EARLY
    lanes = lax.broadcasted_iota(jnp.int32, (1, 128), 1)

    barrier = pltpu.get_barrier_semaphore()

    x, z = g // SIDE, g % SIDE

    def spot(dx, dz):
        return (x + dx) % SIDE * SIDE + (z + dz) % SIDE

    def near(i):
        return i + i // 2

    def greet(graph, leaf):
        pl.semaphore_signal(barrier, inc=1, device_id=(graph, leaf), device_id_type=MESH)

    for i in range(1, SIDE * leaves):
        greet(spot(0, i // leaves), flip(m, i % leaves, leaves))

    for i in range(2 * leaves):
        greet(spot(1 + 2 * (i // leaves), 0), flip(m, i % leaves, leaves))

    for dx, dz in ((2, 0), (1, 1), (1, 3), (3, 1), (3, 3)):
        greet(spot(dx, dz), m)
    greeted = SIDE * leaves - 1 + 2 * leaves + 5

    devices = graphs * leaves
    ids[0] = send_rows[...]
    feats[0] = features[...]

    def leaf_order(i):
        if leaves == 8:
            return i + 2 * ((i // 4) * (1 - 2 * ((i // 2) % 2)))
        return i

    def send_feats(source, p):
        pltpu.make_async_remote_copy(
            src_ref=feats.at[source],
            dst_ref=feats.at[flip(source, p, leaves)],
            send_sem=feat_send,
            recv_sem=feat_recv.at[flip(source, p, leaves)],
            device_id=(g, flip(m, p, leaves)),
            device_id_type=MESH,
        ).start()

    row_lanes = lax.broadcasted_iota(jnp.int32, (1, rows), 1)

    def gather_one(p):
        if p > 0:
            pltpu.make_async_copy(ids.at[p], ids.at[p], ids_recv.at[p]).wait()
            pltpu.make_async_copy(feats.at[p], feats.at[p], feat_recv.at[p]).wait()
            if p % 2 == 0:
                send_feats(p, 1)
        mine = pltpu.roll(ids[p], devices - m, axis=1)
        picked = pick(mine, range(0, devices, leaves), p)
        for target in range(graphs):
            outgoing[target, pl.ds(p * CAP, CAP), :] = picked[target * CAP : (target + 1) * CAP]

    def pick(mine, columns, slot):
        pieces = []
        for column in columns:
            pieces.append((mine[:, column : column + 1] == row_lanes).astype(F32).astype(BF16))
        return jnp.dot(
            jnp.concatenate(pieces, axis=0), feats[slot], preferred_element_type=F32
        ).astype(BF16)

    def send_part(p):
        for i in range(1, 9):
            target = spot(near(i // 3), near(i % 3))
            part = pl.ds(p * CAP, CAP)
            pltpu.make_async_remote_copy(
                src_ref=outgoing.at[target, part],
                dst_ref=arrived.at[g, part],
                send_sem=row_send,
                recv_sem=row_recv.at[g],
                device_id=(target, m),
                device_id_type=MESH,
            ).start()

    opposite = (spot(2, 0), spot(0, 2))

    def send_far_feats(axis):
        slot = leaves + axis
        for ref, send_sem, recv_sem in ((ids, ids_send, ids_recv), (feats, feat_send, feat_recv)):
            pltpu.make_async_remote_copy(
                src_ref=ref.at[0], dst_ref=ref.at[slot], send_sem=send_sem,
                recv_sem=recv_sem.at[slot], device_id=(opposite[axis], m), device_id_type=MESH,
            ).start()

    def gather_far(axis):
        slot = leaves + axis
        pltpu.make_async_copy(ids.at[slot], ids.at[slot], ids_recv.at[slot]).wait()
        pltpu.make_async_copy(feats.at[slot], feats.at[slot], feat_recv.at[slot]).wait()
        if axis == 0:
            mine = pltpu.roll(ids[slot], devices - x * (SIDE * leaves), axis=1)
            stride = leaves
        else:
            mine = pltpu.roll(ids[slot], devices - z * leaves, axis=1)
            stride = SIDE * leaves
        for half in range(2):
            columns = []
            for other in range(2 * half, 2 * half + 2):
                columns.extend(range(other * stride, other * stride + leaves))
            picked = pick(mine, columns, slot)
            for i in range(2 * leaves):
                far[axis, 2 * leaves * half + i] = picked[i * CAP : (i + 1) * CAP]

    def send_far(axis):
        source = opposite[axis]

        def piece(i):
            turn, p = i // leaves, i % leaves
            if axis == 0:
                graph, other = spot(0, turn), (z + turn) % SIDE
            else:
                graph, other = spot(near(turn), 0), (x + near(turn)) % SIDE
            leaf = flip(m, p, leaves)
            part = pl.ds(p * CAP, CAP)
            return far.at[axis, other * leaves + leaf], arrived.at[source, part], graph, leaf

        here, there, _, _ = piece(0)
        pltpu.make_async_copy(here, there, row_recv.at[source]).start()

        for i in range(1, (SIDE - axis) * leaves):
            src, dst, graph, leaf = piece(i)
            pltpu.make_async_remote_copy(
                src_ref=src, dst_ref=dst, send_sem=far_send.at[axis],
                recv_sem=row_recv.at[source], device_id=(graph, leaf), device_id_type=MESH,
            ).start()

    def build_selector():
        @pl.loop(0, groups)
        def _(tg):
            base = pl.multiple_of(tg * GROUP, GROUP)
            node_ids = split_feature[pl.ds(base, GROUP), :]
            cuts = threshold[pl.ds(base, GROUP), :]
            high = cuts.astype(BF16).astype(F32)
            middle = (cuts - high).astype(BF16).astype(F32)
            low = cuts - high - middle
            for node in range(inner):
                column = jnp.broadcast_to(node_ids[:, node : node + 1], (GROUP, 128))
                parts = []
                for q in range(4):
                    parts.append(jnp.where(column == lanes + q * 128, 1.0, 0.0))
                last = parts[3]
                for extra, part in enumerate((high, middle, low)):
                    last = jnp.where(lanes == 64 + extra, -part[:, node : node + 1], last)
                parts[3] = last
                selector[tg, place[node] * GROUP : (place[node] + 1) * GROUP, :] = jnp.concatenate(
                    parts, axis=1
                ).astype(BF16)
            values = leaf_value[pl.ds(base, GROUP), :]
            for pair in range((inner + 1) // 2):
                left = values[:, 2 * pair : 2 * pair + 1]
                right = values[:, 2 * pair + 1 : 2 * pair + 2]
                where = slice(pair * GROUP, (pair + 1) * GROUP)
                scale = 1.0 / (inner + 1)
                leaf_mid[tg, where, :] = jnp.broadcast_to((left + right) * scale, (GROUP, 128))
                leaf_half[tg, where, :] = jnp.broadcast_to((right - left) * scale, (GROUP, 128))

    def start_counts():
        degrees = jnp.broadcast_to(degree[...].astype(F32), (128, rows)).T
        degree_col[...] = degrees
        named_all = jnp.concatenate(
            [neighbour_slot[...], jnp.zeros((128 - entries, rows), jnp.int32)], axis=0
        ).T ^ (m * CAP)
        for j in range(entries):
            named = jnp.broadcast_to(named_all[:, j : j + 1], (rows, 128))
            slot_ids[j] = jnp.where(degrees > j + 0.5, named, -1).astype(jnp.int16)

    def build_counts(first, last):
        one, none = jnp.ones((128, 128), BF16), jnp.zeros((128, 128), BF16)

        @pl.loop(first, last)
        def _(source):
            for half in range(width // 128):
                here = jnp.broadcast_to(lanes + (source * width + half * 128), (128, 128)).astype(
                    jnp.int16
                )
                for part in range(0, rows, 128):
                    total = none
                    for j in range(entries):
                        total = total + jnp.where(slot_ids[j, part : part + 128] == here, one, none)
                    counts[source, part : part + 128, half * 128 : (half + 1) * 128] = total

    def build_rest():
        own_term[...] = (
            jnp.dot(features[...], self_weight[...], preferred_element_type=F32) + hidden_bias[...]
        )
        for place_at, row in enumerate((out_bias, out_gain)):
            wide_row = jnp.concatenate([row[...], jnp.zeros((1, 128 - emb), F32)], axis=1)
            out_cols[place_at] = jnp.broadcast_to(wide_row, (128, 128)).T[:emb]
        for pair in range(leaves // 2):
            emb_t[pair, late_at + emb :, :] = jnp.ones((128 - emb, 2 * rows), BF16)

    def build_margins():
        @pl.loop(0, leaves // 2)
        def _(pair):
            for core in range(2):
                turned = feats[2 * pair + core].T
                where = slice(core * rows, (core + 1) * rows)
                feat_t[:, where] = turned[:EARLY]
                emb_t[pair, 0 : f_in - EARLY, where] = turned[EARLY:]

            for tg in range(groups):
                margins[pair, tg] = jnp.dot(
                    selector[tg, :, :EARLY], feat_t[...], preferred_element_type=F32
                )

    pair_order = (0, 2, 6, 4) if leaves == 8 else tuple(range(0, leaves, 2))
    gather_one(0)
    pl.semaphore_wait(barrier, greeted)

    def send_ids(p):
        pltpu.make_async_remote_copy(
            src_ref=ids.at[0], dst_ref=ids.at[p], send_sem=ids_send, recv_sem=ids_recv.at[p],
            device_id=(g, flip(m, p, leaves)), device_id_type=MESH,
        ).start()

    send_ids(1)
    send_feats(0, 1)
    for axis in range(2):
        send_far_feats(axis)
    send_part(0)

    for i in range(2, leaves):
        send_ids(leaf_order(i))

    for p in pair_order[1:]:
        send_feats(0, p)
    gather_one(1)
    send_part(1)
    build_selector()
    gather_far(0)
    send_far(0)
    start_counts()
    for turn, first in enumerate(pair_order[1:]):
        for p in (first, first + 1):
            gather_one(p)
            send_part(p)
        if turn == 0:
            gather_far(1)
            send_far(1)
        build_counts(turn * 5, turn * 5 + 5)
    build_counts(15, graphs)
    build_rest()
    build_margins()

    summed[...] = jnp.dot(counts[g], outgoing[g], preferred_element_type=F32)

    def add_all(total, sources):
        for source in sources:
            pltpu.make_async_copy(
                arrived.at[source], arrived.at[source], row_recv.at[source]
            ).wait()
        for source in sources:
            total = total + jnp.dot(
                counts[source], arrived[source], preferred_element_type=F32
            )
        return total

    steps = (0, 1, 3)
    summed[...] = add_all(
        summed[...], [spot(2, dz) for dz in range(SIDE)] + [spot(dx, 2) for dx in steps]
    )
    hops = [spot(dx, dz) for dx in steps for dz in steps][1:]
    summed[...] = add_all(summed[...], hops)

    by = jnp.concatenate([degree_col[...]] * (f_in // 128), axis=1)
    mean = (summed[...] / by).astype(BF16)
    hidden = jnp.maximum(
        own_term[...] + jnp.dot(mean, neigh_weight[...], preferred_element_type=F32), 0.0
    ).astype(BF16)
    across = rows // 128
    raw = lax.dot_general(
        out_weight_t[...], hidden, (((1,), (1,)), ((), ())), preferred_element_type=F32
    ) + jnp.concatenate([out_cols[0]] * across, axis=1)
    level = lax.rsqrt(jnp.sum(raw * raw, axis=0, keepdims=True) * (1.0 / emb) + NORM_EPS)
    made_t = raw * level * jnp.concatenate([out_cols[1]] * across, axis=1)
    embedded_t = made_t.astype(BF16)
    emb_t[0, late_at : late_at + emb, 0:rows] = embedded_t

    def emb_slot(p):
        return emb_t.at[p // 2, pl.ds(late_at, emb), pl.ds(p % 2 * rows if isinstance(p, int) else pl.multiple_of(p % 2 * rows, rows), rows)]

    for i in range(1, leaves):
        p = leaf_order(i)
        pltpu.make_async_remote_copy(
            src_ref=emb_slot(0), dst_ref=emb_slot(p), send_sem=emb_send.at[p],
            recv_sem=emb_recv.at[p], device_id=(g, flip(m, p, leaves)), device_id_type=MESH,
        ).start()

    embedding_t[...] = embedded_t

    def one_group(pair, tg):
        late = jnp.dot(selector[tg, :, EARLY:], emb_t[pair], preferred_element_type=F32)

        def value(node, part):
            at = place[node] * GROUP
            if 2 * node + 1 >= inner:
                leaf = node - inner // 2
                low = leaf_mid[tg, leaf * GROUP : (leaf + 1) * GROUP, :]
                gap = leaf_half[tg, leaf * GROUP : (leaf + 1) * GROUP, :]
            else:
                left = value(2 * node + 1, part)
                right = value(2 * node + 2, part)
                low = left + right
                gap = right - left
            where = slice(part * 128, (part + 1) * 128)
            turn = jnp.tanh(
                margins[pair, tg, at : at + GROUP, where] + late[at : at + GROUP, where]
            )
            return low + turn * gap

        for core in range(2):
            for part in range(rows // 128):
                total = value(0, core * (rows // 128) + part)
                where = slice(part * 128, (part + 1) * 128)
                partial[2 * pair + core, :, where] += total[:8] + total[8:]

    def arrive(p):
        pltpu.make_async_copy(emb_slot(p), emb_slot(p), emb_recv.at[p]).wait()

    def leave(p):
        pltpu.make_async_remote_copy(
            src_ref=partial.at[p], dst_ref=partial_in.at[p], send_sem=score_send,
            recv_sem=score_recv.at[p], device_id=(g, flip(m, p, leaves)), device_id_type=MESH,
        ).start()

    partial[...] = jnp.zeros(partial.shape, F32)

    @pl.loop(0, leaves // 2)
    def _(i):
        pair = leaf_order(2 * i) // 2

        @pl.when(i > 0)
        def _():
            arrive(2 * pair)

        arrive(2 * pair + 1)
        for tg in range(groups):
            one_group(pair, tg)

        @pl.when(i > 0)
        def _():
            leave(2 * pair)

        leave(2 * pair + 1)

    running = partial[0]
    for p in range(1, leaves):
        pltpu.make_async_copy(partial_in.at[p], partial_in.at[p], score_recv.at[p]).wait()
        running = running + partial_in[p]
    scores[...] = jnp.sum(running, axis=0, keepdims=True)

    others = pl.ds(0, leaves + 1)
    pltpu.make_async_copy(ids.at[others], ids.at[others], ids_send).wait()
    pltpu.make_async_copy(feats.at[others], feats.at[others], feat_send).wait()
    for axis in range(2):
        block = far.at[axis, pl.ds(0, (SIDE - axis) * leaves - 1)]
        pltpu.make_async_copy(block, block, far_send.at[axis]).wait()
    block = outgoing.at[pl.ds(0, 8)]
    pltpu.make_async_copy(block, block, row_send).wait()
    for p in range(1, leaves):
        pltpu.make_async_copy(emb_slot(p), emb_slot(p), emb_send.at[p]).wait()
    block = partial.at[pl.ds(0, leaves - 1)]
    pltpu.make_async_copy(block, block, score_send).wait()


def on_device(
    graphs,
    leaves,
    features,
    send_rows,
    neighbour_slot,
    degree,
    self_weight,
    neigh_weight,
    hidden_bias,
    out_weight,
    out_bias,
    out_gain,
    split_feature,
    threshold,
    leaf_value,
):
    rows, f_in = features.shape
    hid = self_weight.shape[1]
    emb = out_weight.shape[1]
    trees, inner = split_feature.shape
    groups = trees // GROUP
    width = leaves * CAP
    entries = neighbour_slot.shape[1]
    dma = pltpu.SemaphoreType.DMA
    vmem = pl.BlockSpec(memory_space=pltpu.VMEM)
    embedding_t, scores = pl.pallas_call(
        functools.partial(kernel, graphs, leaves),
        out_shape=(
            pltpu.VMEM((emb, rows), BF16),
            pltpu.VMEM((1, rows), F32),
        ),
        in_specs=[vmem] * 13,
        out_specs=(vmem, vmem),
        scratch_shapes=[
            pltpu.VMEM((leaves + 2, rows, f_in), BF16),
            pltpu.VMEM((leaves + 2, CAP, graphs * leaves), jnp.int32),
            pltpu.VMEM((graphs, width, f_in), BF16),
            pltpu.VMEM((2, SIDE * leaves, CAP, f_in), BF16),
            pltpu.VMEM((graphs, width, f_in), BF16),
            pltpu.VMEM((entries, rows, 128), jnp.int16),
            pltpu.VMEM((graphs, rows, width), BF16),
            pltpu.VMEM((groups, inner * GROUP, 512), BF16),
            pltpu.VMEM((groups, (inner + 1) // 2 * GROUP, 128), F32),
            pltpu.VMEM((groups, (inner + 1) // 2 * GROUP, 128), F32),
            pltpu.VMEM((EARLY, 2 * rows), BF16),
            pltpu.VMEM((leaves // 2, 512 - EARLY, 2 * rows), BF16),
            pltpu.VMEM((leaves // 2, groups, inner * GROUP, 2 * rows), F32),
            pltpu.VMEM((rows, hid), F32),
            pltpu.VMEM((2, emb, 128), F32),
            pltpu.VMEM((rows, 128), F32),
            pltpu.VMEM((rows, f_in), F32),
            pltpu.VMEM((leaves, 8, rows), F32),
            pltpu.VMEM((leaves, 8, rows), F32),
            dma,
            dma,
            dma,
            dma((2,)),
            dma((leaves,)),
            dma,
            dma((leaves + 2,)),
            dma((leaves + 2,)),
            dma((graphs,)),
            dma((leaves,)),
            dma((leaves,)),
        ],
        compiler_params=pltpu.CompilerParams(
            collective_id=0, has_side_effects=True, vmem_limit_bytes=62 * 2**20
        ),
        name="sage_forest",
    )(
        features,
        send_rows.reshape(send_rows.shape[1:]).T,
        neighbour_slot.T,
        degree.reshape(1, rows),
        self_weight,
        neigh_weight,
        hidden_bias.reshape(1, hid),
        out_weight.T,
        out_bias.reshape(1, emb),
        out_gain.reshape(1, emb),
        split_feature,
        threshold,
        leaf_value,
    )
    return (embedding_t.T, scores.reshape(rows))


def solution(mesh):
    in_specs = (
        P(("graph", "leaf"), None),
        P(("graph", "leaf"), None, None),
        P(("graph", "leaf"), None),
        P(("graph", "leaf")),
        P(),
        P(),
        P(),
        P(),
        P(),
        P(),
        P("leaf", None),
        P("leaf", None),
        P("leaf", None),
    )
    out_specs = (P(("graph", "leaf"), None), P(("graph", "leaf")))
    return jax.shard_map(
        functools.partial(on_device, mesh.shape["graph"], mesh.shape["leaf"]),
        mesh=mesh,
        in_specs=in_specs,
        out_specs=out_specs,
        check_vma=False,
    )
```
